32 devices in a mesh: fsdp: 2 (over x), ctx: 4 (over y, core), tp: 4 (over z).
Axes of the slice: x: 2, y: 2, z: 4, core: 2. Of those that a mesh axis runs over, the one named last changes fastest.
Arguments:
- tokens: bfloat16 [2, 2048, 2304], P('fsdp', 'ctx'), may hold values from -6 to 6
- q_weight: bfloat16 [2304, 2048], P(('fsdp', 'ctx'), 'tp'), as said below
- key_weight: bfloat16 [2304, 1024], P(('fsdp', 'ctx'), 'tp'), may hold values from -0.125 to 0.125
- value_weight: bfloat16 [2304, 1024], P(('fsdp', 'ctx'), 'tp'), may hold values from -0.125 to 0.125
- out_weight: bfloat16 [2048, 2304], P('tp', ('fsdp', 'ctx')), may hold values from -0.125 to 0.125
- gate_weight: bfloat16 [2304, 9216], P(('fsdp', 'ctx'), 'tp'), may hold values from -0.125 to 0.125
- up_weight: bfloat16 [2304, 9216], P(('fsdp', 'ctx'), 'tp'), may hold values from -0.125 to 0.125
- down_weight: bfloat16 [9216, 2304], P('tp', ('fsdp', 'ctx')), may hold values from -0.0625 to 0.0625
- gain_attn_in: bfloat16 [2304], P(('fsdp', 'ctx')), may hold values from 0.099609375 to 1.8984375
- gain_attn_out: bfloat16 [2304], P(('fsdp', 'ctx')), may hold values from 0.099609375 to 1.8984375
- gain_mlp_in: bfloat16 [2304], P(('fsdp', 'ctx')), may hold values from 0.099609375 to 1.8984375
- gain_mlp_out: bfloat16 [2304], P(('fsdp', 'ctx')), may hold values from 0.099609375 to 1.8984375
- segment_ids: int32 [2, 2048], P('fsdp'), may hold values from 0 to 4, as said below
- block_order: int32 [2, 8], P('fsdp'), may hold values from 0 to 7, as said below
- cotangent: bfloat16 [2, 2048, 2304], P('fsdp', 'ctx'), may hold values from -6 to 6
Outputs:
- layer_out: bfloat16 [2, 2048, 2304], P('fsdp', 'ctx')
- grad_tokens: float32 [2, 2048, 2304], P('fsdp', 'ctx')
- grad_q_weight: float32 [2304, 2048], P(('fsdp', 'ctx'), 'tp')
- grad_key_weight: float32 [2304, 1024], P(('fsdp', 'ctx'), 'tp')
- grad_value_weight: float32 [2304, 1024], P(('fsdp', 'ctx'), 'tp')
- grad_out_weight: float32 [2048, 2304], P('tp', ('fsdp', 'ctx'))
- grad_gate_weight: float32 [2304, 9216], P(('fsdp', 'ctx'), 'tp')
- grad_up_weight: float32 [2304, 9216], P(('fsdp', 'ctx'), 'tp')
- grad_down_weight: float32 [9216, 2304], P('tp', ('fsdp', 'ctx'))
- grad_gain_attn_in: float32 [2304], P(('fsdp', 'ctx'))
- grad_gain_attn_out: float32 [2304], P(('fsdp', 'ctx'))
- grad_gain_mlp_in: float32 [2304], P(('fsdp', 'ctx'))
- grad_gain_mlp_out: float32 [2304], P(('fsdp', 'ctx'))
The draws below stay inside these ranges and needn't reach their ends.
Inputs may be any that keep to these rules, and one draw needn't show every extreme that they name: `segment_ids`: along each sequence the ids never fall; every one of the 5 documents is present; document 0 covers at least the first 1024 positions. `block_order`: each row is a permutation of the 8 blocks; stored blocks 2j and 2j + 1 hold true blocks b and 7 - b for some b. `q_weight`: every entry is at most 24 / sqrt(2304) in magnitude.
All inputs are finite; a program needn't handle non-finite values.
Results may differ from the reference program's by a relative error of at most 0.023.
The reference program's roundings to bfloat16 on the way count: a program that leaves them out, or rounds other values in their place, can miss the bound.
Values may be sent and summed in bfloat16 or wider, within the bound.
No kernel may reach another device: no remote copies, remote signals or barrier semaphores. Data moves between devices by JAX's collectives and lax.ppermute only.
A program may use at most 256 MiB of HBM per device.

```python
import jax
import jax.numpy as jnp
from jax import lax

D = 2304
HEADS = 8
KV_HEADS = 4
HEAD_DIM = 256
FF = 9216
BLOCK = 256
DOCS = 5
SEQ_LEN = 2048
SEQS = 2
NBLK = 8


def draw_segment_ids(key, part):
    key = jax.random.fold_in(key, 7)
    seq_keys = jax.random.split(key, SEQS)

    def single_sequence(subkey):
        boundary = jax.random.permutation(subkey, SEQ_LEN // 2)[:DOCS - 1] + SEQ_LEN // 2
        places = jnp.arange(SEQ_LEN, dtype=jnp.int32)
        return jnp.sum((places[:, None] >= boundary[None, :]).astype(jnp.int32), axis=1)
    return jax.vmap(single_sequence)(seq_keys).astype(jnp.int32)


def draw_block_order(key, part):
    key = jax.random.fold_in(key, 13)
    seq_keys = jax.random.split(key, SEQS)

    def single_sequence(subkey):
        first_key, second_key = jax.random.split(subkey)
        pairing = jax.random.permutation(first_key, NBLK // 2)
        flipped = jax.random.randint(second_key, (NBLK // 2,), 0, 2)
        leading = jnp.where(flipped == 1, NBLK - 1 - pairing, pairing)
        return jnp.stack([leading, NBLK - 1 - leading], axis=1).reshape(NBLK)
    return jax.vmap(single_sequence)(seq_keys).astype(jnp.int32)


def draw_q_weight(key, part):
    key = jax.random.fold_in(key, 21)
    rank_key, entry_key = jax.random.split(key)
    ranks = jax.random.permutation(rank_key, HEADS).astype(jnp.float32)
    factors = 6.0 ** (ranks / (HEADS - 1))
    columns = jnp.repeat(factors, HEAD_DIM)
    entries = jnp.clip(jax.random.normal(entry_key, (D, HEADS * HEAD_DIM), jnp.float32), -4.0, 4.0)
    return (entries * columns[None, :] / jnp.sqrt(jnp.float32(D))).astype(jnp.bfloat16)


def steps_of(stream_key, shape, cuts, low, high):
    level = 1.0
    for position, shards_of in cuts:
        draws = jax.random.uniform(jax.random.fold_in(jax.random.fold_in(stream_key, 6), position), (shards_of,), jnp.float32, low / len(cuts), high / len(cuts))
        level = level * jnp.repeat(jnp.exp(draws), shape[position] // shards_of).reshape((-1,) + (1,) * (len(shape) - 1 - position))
    return level


def noise(rng, shape, spread, reach, cuts=(), kind=jnp.bfloat16):
    array = spread * jax.random.normal(rng, shape, jnp.float32)
    if cuts:
        array = array * steps_of(rng, shape, cuts, -0.22, 0.18)
    return jnp.clip(array, -reach, reach).astype(kind)


def setup_inputs(seed: int = 0) -> dict:
    streams_of = jax.random.split(jax.random.key(seed), 16)
    tokens = noise(streams_of[0], (SEQS, SEQ_LEN, D), 1.0, 6.0, ((0, 2), (1, 4)))
    q_weight = draw_q_weight(jax.random.fold_in(streams_of[15], 71), 0)
    key_weight = noise(streams_of[2], (D, KV_HEADS * HEAD_DIM), D ** -0.5, 0.125, ((0, 8), (1, 4)))
    value_weight = noise(streams_of[3], (D, KV_HEADS * HEAD_DIM), D ** -0.5, 0.125, ((0, 8), (1, 4)))
    out_weight = noise(streams_of[4], (HEADS * HEAD_DIM, D), (HEADS * HEAD_DIM) ** -0.5, 0.125, ((0, 4), (1, 8)))
    gate_weight = noise(streams_of[5], (D, FF), D ** -0.5, 0.125, ((0, 8), (1, 4)))
    up_weight = noise(streams_of[6], (D, FF), D ** -0.5, 0.125, ((0, 8), (1, 4)))
    down_weight = noise(streams_of[7], (FF, D), FF ** -0.5, 0.0625, ((0, 4), (1, 8)))
    gain_attn_in = jnp.clip(1.0 + 0.18 * jax.random.normal(streams_of[8], (D,), jnp.float32), 0.099609375, 1.8984375).astype(jnp.bfloat16)
    gain_attn_out = jnp.clip(1.0 + 0.18 * jax.random.normal(streams_of[9], (D,), jnp.float32), 0.099609375, 1.8984375).astype(jnp.bfloat16)
    gain_mlp_in = jnp.clip(1.0 + 0.18 * jax.random.normal(streams_of[10], (D,), jnp.float32), 0.099609375, 1.8984375).astype(jnp.bfloat16)
    gain_mlp_out = jnp.clip(1.0 + 0.18 * jax.random.normal(streams_of[11], (D,), jnp.float32), 0.099609375, 1.8984375).astype(jnp.bfloat16)
    segment_ids = draw_segment_ids(jax.random.fold_in(streams_of[15], 71), 0)
    block_order = draw_block_order(jax.random.fold_in(streams_of[15], 71), 0)
    cotangent = noise(streams_of[14], (SEQS, SEQ_LEN, D), 1.0, 6.0, ((0, 2), (1, 4)))
    return {"tokens": tokens, "q_weight": q_weight, "key_weight": key_weight, "value_weight": value_weight, "out_weight": out_weight, "gate_weight": gate_weight, "up_weight": up_weight, "down_weight": down_weight, "gain_attn_in": gain_attn_in, "gain_attn_out": gain_attn_out, "gain_mlp_in": gain_mlp_in, "gain_mlp_out": gain_mlp_out, "segment_ids": segment_ids, "block_order": block_order, "cotangent": cotangent}


EPS = 1e-06
CAP = 50.0
THETA = 10000.0

@jax.custom_vjp
def low(v):
    return lax.optimization_barrier(v.astype(jnp.bfloat16)).astype(jnp.float32)

@jax.custom_vjp
def low_back(v):
    return v

def low_keep(v):
    return (low(v), None)

def low_pass(kept, grad):
    return (grad,)

def back_keep(v):
    return (v, None)

def back_low(kept, grad):
    return (low(grad),)
low.defvjp(low_keep, low_pass)
low_back.defvjp(back_keep, back_low)

def matmul(left, right):
    return jnp.dot(left, right, precision=lax.Precision.HIGHEST, preferred_element_type=jnp.float32)

def norm(values, gain):
    return values * lax.rsqrt(lax.optimization_barrier(jnp.mean(values * values, axis=-1, keepdims=True)) + EPS) * gain

def rotate(values, positions):
    half = values.shape[-1] // 2
    freqs = THETA ** (-jnp.arange(half, dtype=jnp.float32) * 2.0 / values.shape[-1])
    angles = positions.astype(jnp.float32)[:, None] * freqs[None, :]
    cosine = jnp.cos(angles)[:, None, :]
    sine = jnp.sin(angles)[:, None, :]
    first = values[..., :half]
    second = values[..., half:]
    return jnp.concatenate([first * cosine - second * sine, second * cosine + first * sine], axis=-1)

def attend_sequence(queries, keys, values, positions, segments):
    rows = min(512, SEQ_LEN)
    keys_wide = jnp.repeat(keys, HEADS // KV_HEADS, axis=1)
    values_wide = jnp.repeat(values, HEADS // KV_HEADS, axis=1)

    def block_step(item):
        query_block, pos_block, seg_block = item
        scores = low_back(jnp.einsum('rhd,khd->hrk', query_block, keys_wide, precision=lax.Precision.HIGHEST))
        capped = CAP * jnp.tanh(scores / CAP)
        allowed = (seg_block[:, None] == segments[None, :]) & ((pos_block // BLOCK)[:, None] >= (positions // BLOCK)[None, :])
        masked = jnp.where(allowed[None], capped, -1e+30)
        highest = lax.optimization_barrier(jnp.max(masked, axis=-1, keepdims=True))
        expo = jnp.exp(masked - highest)
        probs = low(expo / lax.optimization_barrier(jnp.sum(expo, axis=-1, keepdims=True)))
        return jnp.einsum('hrk,khd->rhd', probs, values_wide, precision=lax.Precision.HIGHEST)
    result = lax.map(jax.checkpoint(block_step), (queries.reshape(-1, rows, HEADS, HEAD_DIM), positions.reshape(-1, rows), segments.reshape(-1, rows)))
    return result.reshape(SEQ_LEN, HEADS, HEAD_DIM)

def reference(tokens, q_weight, key_weight, value_weight, out_weight, gate_weight, up_weight, down_weight, gain_attn_in, gain_attn_out, gain_mlp_in, gain_mlp_out, segment_ids, block_order, cotangent):
    within = jnp.arange(BLOCK, dtype=jnp.int32)
    positions = (block_order[:, :, None] * BLOCK + within[None, None, :]).reshape(SEQS, SEQ_LEN).astype(jnp.int32)
    segments = jnp.take_along_axis(segment_ids, positions, axis=1)
    flat_pos = positions.reshape(-1)

    def forward(tokens_in, q_mat, key_mat, value_mat, out_mat, gate_mat, up_mat, down_mat, gain_one, gain_two, gain_three, gain_four):
        flat = tokens_in.reshape(SEQS * SEQ_LEN, D)
        normed_attn = low(norm(flat, gain_one))
        queries = low(rotate(low_back(matmul(normed_attn, q_mat)).reshape(-1, HEADS, HEAD_DIM), flat_pos) * HEAD_DIM ** (-0.5))
        keys = low(rotate(low_back(matmul(normed_attn, key_mat)).reshape(-1, KV_HEADS, HEAD_DIM), flat_pos))
        values = low(low_back(matmul(normed_attn, value_mat))).reshape(-1, KV_HEADS, HEAD_DIM)
        pieces = []
        for sequence in range(SEQS):
            lower = sequence * SEQ_LEN
            upper = lower + SEQ_LEN
            pieces.append(attend_sequence(queries[lower:upper], keys[lower:upper], values[lower:upper], positions[sequence], segments[sequence]))
        attended = low(low_back(jnp.concatenate(pieces, axis=0).reshape(-1, HEADS * HEAD_DIM)))
        branch_attn = low_back(matmul(attended, out_mat))
        resid = flat + norm(branch_attn, gain_two)
        normed_mlp = low(norm(resid, gain_three))
        gate_lin = low_back(matmul(normed_mlp, gate_mat))
        up_lin = low_back(matmul(normed_mlp, up_mat))
        activ = low(jax.nn.gelu(gate_lin, approximate=True) * up_lin)
        branch_mlp = low_back(matmul(activ, down_mat))
        return (resid + norm(branch_mlp, gain_four)).reshape(SEQS, SEQ_LEN, D)
    floats = [item.astype(jnp.float32) for item in (tokens, q_weight, key_weight, value_weight, out_weight, gate_weight, up_weight, down_weight, gain_attn_in, gain_attn_out, gain_mlp_in, gain_mlp_out)]
    layer_out, pullback = jax.vjp(forward, *floats)
    grads = pullback(cotangent.astype(jnp.float32))
    return (layer_out.astype(jnp.bfloat16), grads[0], grads[1], grads[2], grads[3], grads[4], grads[5], grads[6], grads[7], grads[8], grads[9], grads[10], grads[11])
```

```python
import functools

import jax
import jax.numpy as jnp
import numpy as np
from jax import lax
from jax.experimental import pallas as pl
from jax.experimental.pallas import tpu as pltpu
from jax.sharding import PartitionSpec as P

HEAD_DIM = 256
BLOCK = 256
EPS = 1e-06
CAP = 50.0
THETA = 10000.0
F32 = jnp.float32
BF16 = jnp.bfloat16


class Ring:
    def __init__(self, sizes, axes):
        self.axes = axes
        outer = sizes[axes[0]] if len(axes) == 2 else 1
        inner = sizes[axes[-1]] // 2
        order = []
        for row in range(outer):
            cols = range(inner) if row % 2 == 0 else reversed(range(inner))
            order += [row * inner + col for col in cols]
        self.order = np.array(order, np.int32)
        self.count = len(order)
        self.place = np.argsort(self.order).astype(np.int32)
        self.sibling = [(i, i ^ 1) for i in range(2 * self.count)]

    def pairs(self, sign):
        out = []
        for pos in range(self.count):
            for core in range(2):
                step = sign if core == 0 else -sign
                there = self.order[(pos + step) % self.count]
                out.append((int(self.order[pos]) * 2 + core, int(there) * 2 + core))
        return out

    def locate(self):
        me = lax.axis_index(self.axes)
        core = me % 2
        pos = jnp.asarray(self.place)[me // 2]
        return pos, core

    def owner(self, pos, core, label):
        step = jnp.where(core == 0, label, -label)
        return jnp.asarray(self.order)[(pos + step) % self.count] * 2 + core

    def swap(self, value):
        return lax.ppermute(value, self.axes, self.sibling)


def put(buffer, piece, index):
    starts = (index * piece.shape[0],) + (0,) * (buffer.ndim - 1)
    return lax.dynamic_update_slice(buffer, piece, starts)


def gather(ring, shard):
    pos, core = ring.locate()
    whole = jnp.zeros((2 * ring.count * shard.shape[0],) + shard.shape[1:], shard.dtype)
    piece = shard
    for label in range(ring.count):
        if label:
            piece = lax.ppermute(piece, ring.axes, ring.pairs(-1))
        other = ring.swap(piece)
        whole = put(whole, piece, ring.owner(pos, core, label))
        whole = put(whole, other, ring.owner(pos, 1 - core, label))
    return whole


def scatter(ring, value, wire):
    pos, core = ring.locate()
    rows = value.shape[0] // (2 * ring.count)

    def block(kind, label):
        start = ring.owner(pos, kind, label) * rows
        return lax.dynamic_slice_in_dim(value, start, rows).astype(wire)

    def both(label):
        count = ring.count
        theirs = block(1 - core, label)
        return block(core, label % count).astype(F32) + ring.swap(theirs).astype(F32)

    total = both(ring.count - 1) if ring.count > 1 else both(0)
    for label in range(ring.count - 2, -1, -1):
        got = lax.ppermute(total.astype(wire), ring.axes, ring.pairs(1))
        total = both(label) + got.astype(F32)
    return total


def tp_pairs(count):
    return [(i, (i + 1) % count) for i in range(count)]


def tp_scatter(part, count):
    here = lax.axis_index("tp")
    rows = part.shape[0] // count

    def chunk(back):
        return lax.dynamic_slice_in_dim(part, ((here - back) % count) * rows, rows)

    total = chunk(1).astype(F32)
    for step in range(1, count):
        got = lax.ppermute(total.astype(BF16), "tp", tp_pairs(count))
        total = chunk(step + 1).astype(F32) + got.astype(F32)
    return total


def tp_gather(own, count):
    here = lax.axis_index("tp")
    whole = put(jnp.zeros((count * own.shape[0],) + own.shape[1:], own.dtype), own, here)
    piece = own
    for step in range(1, count):
        piece = lax.ppermute(piece, "tp", tp_pairs(count))
        whole = put(whole, piece, (here - step) % count)
    return whole


def inverse_of(values):
    return lax.rsqrt(jnp.mean(values * values, axis=-1, keepdims=True) + EPS)


def norm_back(values, inverse, gain, upstream):
    scaled = upstream * gain
    d_values = inverse * scaled - values * (
        inverse * inverse * inverse * jnp.mean(scaled * values, axis=-1, keepdims=True)
    )
    return d_values, jnp.sum(upstream * values * inverse, axis=0)


def rotate(values, cosine, sine):
    half = values.shape[-1] // 2
    first, second = values[..., :half], values[..., half:]
    return jnp.concatenate(
        [first * cosine - second * sine, second * cosine + first * sine], axis=-1
    )


def dot(left, right):
    return jnp.dot(left, right, preferred_element_type=F32)


def dot_nt(left, right):
    return lax.dot_general(left, right, (((1,), (1,)), ((), ())), preferred_element_type=F32)


def dot_tn(left, right):
    return lax.dot_general(left, right, (((0,), (0,)), ((), ())), preferred_element_type=F32)


GELU_A = 0.7978845608028654
GELU_B = 0.044715


def gelu(gate):
    return 0.5 * gate * (1.0 + jnp.tanh(GELU_A * (gate + GELU_B * gate * gate * gate)))


def gelu_and_slope(gate):
    square = gate * gate
    bent = jnp.tanh(GELU_A * (gate + GELU_B * gate * square))
    half = 0.5 * (1.0 + bent)
    slope = half + 0.5 * gate * (1.0 - bent * bent) * GELU_A * (1.0 + 3.0 * GELU_B * square)
    return gate * half, slope


def stack_heads(ref, rows, first, count):
    return jnp.concatenate(
        [ref[rows, pl.ds((first + h) * HEAD_DIM, HEAD_DIM)] for h in range(count)], axis=0
    )


def attend_kernel(heads, info, q_ref, kv_ref, qseg_ref, kseg_ref, out_ref, inv_ref, p_ref):
    low, high = info[0], info[1]
    rows = heads * BLOCK
    every = pl.ds(0, BLOCK)
    query = stack_heads(q_ref, every, 0, heads)
    qseg = jnp.concatenate([qseg_ref[...]] * heads, axis=0)

    def first(j, acc):
        start = pl.multiple_of(info[2 + j] * BLOCK, BLOCK)
        scores = dot_nt(query, kv_ref[pl.ds(start, BLOCK), pl.ds(0, HEAD_DIM)])
        weight = jnp.exp(CAP * jnp.tanh(scores * (1.0 / CAP)))
        weight = jnp.where(qseg == kseg_ref[pl.ds(j, 1), :], weight, 0.0)
        p_ref[j] = weight
        return acc + weight[:, :128] + weight[:, 128:]

    acc = lax.fori_loop(low, high + 1, first, jnp.zeros((rows, 128), F32))
    inverse = 1.0 / jnp.sum(acc, axis=1, keepdims=True)
    inv_ref[...] = inverse

    def second(j, total):
        start = pl.multiple_of(info[2 + j] * BLOCK, BLOCK)
        low_probs = (p_ref[j] * inverse).astype(BF16)
        return total + dot(low_probs, kv_ref[pl.ds(start, BLOCK), pl.ds(HEAD_DIM, HEAD_DIM)])

    total = lax.fori_loop(low, high + 1, second, jnp.zeros((rows, HEAD_DIM), F32))
    for h in range(heads):
        out_ref[:, pl.ds(h * HEAD_DIM, HEAD_DIM)] = total[h * BLOCK : (h + 1) * BLOCK].astype(BF16)


def vmem():
    return pl.BlockSpec(memory_space=pltpu.VMEM)


def attend(info, queries, kv, qseg, kseg, heads):
    blocks = kseg.shape[0]
    return pl.pallas_call(
        functools.partial(attend_kernel, heads),
        out_shape=(
            jax.ShapeDtypeStruct((BLOCK, heads * HEAD_DIM), BF16),
            jax.ShapeDtypeStruct((heads * BLOCK, 1), F32),
        ),
        in_specs=[pl.BlockSpec(memory_space=pltpu.SMEM)] + [vmem()] * 4,
        out_specs=(vmem(), vmem()),
        scratch_shapes=[pltpu.VMEM((blocks, heads * BLOCK, BLOCK), F32)],
        compiler_params=pltpu.CompilerParams(vmem_limit_bytes=(24 if blocks <= 8 else 48) << 20),
        cost_estimate=pl.CostEstimate(
            flops=3 * heads * BLOCK * blocks * BLOCK * HEAD_DIM,
            bytes_accessed=4 << 20,
            transcendentals=heads * BLOCK * blocks * BLOCK,
        ),
        name="attend",
    )(info, queries, kv, qseg, kseg)


def attend_back_kernel(
    heads, each, info, q_ref, do_ref, kv_ref, inv_ref, qseg_ref, kseg_ref, dq_ref, dkv_ref,
    p_ref, g_ref, dp_ref,
):
    blocks_q = q_ref.shape[0] // BLOCK
    dkv_ref[...] = jnp.zeros(dkv_ref.shape, F32)
    keys = pl.ds(0, HEAD_DIM)
    vals = pl.ds(HEAD_DIM, HEAD_DIM)
    for i in range(blocks_q):
        low, high = info[2 * i], info[2 * i + 1]
        qrows = pl.ds(i * BLOCK, BLOCK)
        qseg = jnp.concatenate([qseg_ref[qrows, :]] * each, axis=0)
        for h in range(0, heads, each):
            query = stack_heads(q_ref, qrows, h, each)
            d_out = stack_heads(do_ref, qrows, h, each)
            inverse = inv_ref[pl.ds((i * heads + h) * BLOCK, each * BLOCK), :]

            def first(j, acc, query=query, d_out=d_out, inverse=inverse, qseg=qseg):
                start = pl.multiple_of(info[2 * blocks_q + j] * BLOCK, BLOCK)
                place = pl.ds(start, BLOCK)
                bent = jnp.tanh(dot_nt(query, kv_ref[place, keys]) * (1.0 / CAP))
                probs = jnp.exp(CAP * bent) * inverse
                probs = jnp.where(qseg == kseg_ref[pl.ds(j, 1), :], probs, 0.0)
                d_probs = dot_nt(d_out, kv_ref[place, vals])
                p_ref[j] = probs.astype(BF16)
                g_ref[j] = probs * (1.0 - bent * bent)
                dp_ref[j] = d_probs
                both = probs * d_probs
                return acc + both[:, :128] + both[:, 128:]

            acc = lax.fori_loop(low, high + 1, first, jnp.zeros((each * BLOCK, 128), F32))
            inner = jnp.sum(acc, axis=1, keepdims=True)

            def second(j, total, query=query, d_out=d_out, inner=inner):
                start = pl.multiple_of(info[2 * blocks_q + j] * BLOCK, BLOCK)
                place = pl.ds(start, BLOCK)
                d_scores = (g_ref[j] * (dp_ref[j] - inner)).astype(BF16)
                dkv_ref[place, keys] += dot_tn(d_scores, query)
                dkv_ref[place, vals] += dot_tn(p_ref[j], d_out)
                return total + dot(d_scores, kv_ref[place, keys])

            total = lax.fori_loop(
                low, high + 1, second, jnp.zeros((each * BLOCK, HEAD_DIM), F32)
            )
            for n in range(each):
                dq_ref[qrows, pl.ds((h + n) * HEAD_DIM, HEAD_DIM)] = total[
                    n * BLOCK : (n + 1) * BLOCK
                ]


def attend_back(info, queries, d_out, kv, inverse, qseg, kseg, heads):
    blocks = kseg.shape[0]
    each = heads if blocks <= 8 else 1
    tile = (blocks, each * BLOCK, BLOCK)
    return pl.pallas_call(
        functools.partial(attend_back_kernel, heads, each),
        out_shape=(
            jax.ShapeDtypeStruct(queries.shape, F32),
            jax.ShapeDtypeStruct(kv.shape, F32),
        ),
        in_specs=[pl.BlockSpec(memory_space=pltpu.SMEM)] + [vmem()] * 6,
        out_specs=(vmem(), vmem()),
        scratch_shapes=[pltpu.VMEM(tile, BF16), pltpu.VMEM(tile, F32), pltpu.VMEM(tile, F32)],
        compiler_params=pltpu.CompilerParams(vmem_limit_bytes=(32 if blocks <= 8 else 56) << 20),
        cost_estimate=pl.CostEstimate(
            flops=11 * heads * BLOCK * blocks * BLOCK * HEAD_DIM,
            bytes_accessed=10 << 20,
            transcendentals=2 * heads * BLOCK * blocks * BLOCK,
        ),
        name="attend_back",
    )(info, queries, d_out, kv, inverse, qseg, kseg)


def per_device(
    sizes,
    tokens,
    q_weight,
    key_weight,
    value_weight,
    out_weight,
    gate_weight,
    up_weight,
    down_weight,
    gain_attn_in,
    gain_attn_out,
    gain_mlp_in,
    gain_mlp_out,
    segment_ids,
    block_order,
    cotangent,
):
    tp = sizes["tp"]
    wide = Ring(sizes, ("fsdp", "ctx"))
    near = Ring(sizes, ("ctx",))
    group = 2 * wide.count
    here = lax.axis_index("tp")
    tok = tokens[0]
    count, width = tok.shape
    halves = count // BLOCK
    share = BLOCK // tp
    heads = q_weight.shape[1] // HEAD_DIM
    qcols = q_weight.shape[1]

    qkv_w = gather(wide, jnp.concatenate([q_weight, key_weight, value_weight], axis=1))
    out_w = gather(wide, out_weight.T)
    gains_own = jnp.stack([gain_attn_in, gain_attn_out, gain_mlp_in, gain_mlp_out])
    gains = gather(wide, gains_own[None]).astype(F32)
    gains = gains.transpose(1, 0, 2).reshape(4, width)
    gain_one, gain_two, gain_three, gain_four = (gains[i] for i in range(4))
    gate_w = gather(wide, gate_weight)
    up_w = gather(wide, up_weight)
    down_w = gather(wide, down_weight.T)

    order = block_order[0]
    blocks = order.shape[0]
    stored = jnp.argsort(order).astype(jnp.int32)
    segs = segment_ids[0].reshape(blocks, BLOCK)
    first_block = lax.axis_index("ctx") * halves
    high = lax.dynamic_slice_in_dim(order, first_block, halves)
    qsegs = segs[high]
    low = jnp.sum((segs[None, :, -1] < qsegs[:, :1]).astype(jnp.int32), axis=1)
    bounds = jnp.stack([low, high], axis=1).astype(jnp.int32)
    infos = [jnp.concatenate([bounds[i], stored]) for i in range(halves)]
    info_all = jnp.concatenate([bounds.reshape(-1), stored])
    qseg = qsegs.reshape(count, 1)

    spot = (high[:, None] * BLOCK + jnp.arange(BLOCK, dtype=jnp.int32)[None]).reshape(-1)
    half_dim = HEAD_DIM // 2
    freqs = THETA ** (-jnp.arange(half_dim, dtype=F32) * 2.0 / HEAD_DIM)
    angles = spot.astype(F32)[:, None] * freqs[None, :]
    cosine, sine = jnp.cos(angles), jnp.sin(angles)
    scale = HEAD_DIM**-0.5

    inputs = tok.astype(F32)
    inv_one = inverse_of(inputs)
    normed_attn = (inputs * inv_one * gain_one).astype(BF16)
    lin = dot(normed_attn, qkv_w)
    q_lin = lin[:, :qcols].reshape(count, heads, HEAD_DIM)
    queries = (rotate(q_lin, cosine[:, None], sine[:, None]) * scale).astype(BF16)
    queries = queries.reshape(count, qcols)
    keys = rotate(lin[:, qcols : qcols + HEAD_DIM], cosine, sine).astype(BF16)
    values = lin[:, qcols + HEAD_DIM :].astype(BF16)
    kv = gather(near, jnp.concatenate([keys, values], axis=1))

    def rows_of(array, i):
        return lax.slice_in_dim(array, i * BLOCK, (i + 1) * BLOCK)

    def share_of(array, i):
        return lax.dynamic_slice_in_dim(array, i * BLOCK + here * share, share).astype(F32)

    attended, inverse_sum, branch_attn, inv_two, resid, inv_three, normed_mlp = ([] for _ in range(7))
    for i in range(halves):
        out, inv = attend(infos[i], rows_of(queries, i), kv, rows_of(qseg, i), segs, heads)
        attended.append(out)
        inverse_sum.append(inv)
        branch = tp_scatter(dot_nt(out, out_w), tp)
        branch_attn.append(branch)
        inv_two.append(inverse_of(branch))
        resid.append(share_of(tok, i) + branch * inv_two[i] * gain_two)
        inv_three.append(inverse_of(resid[i]))
        normed_mlp.append(tp_gather((resid[i] * inv_three[i] * gain_three).astype(BF16), tp))

    gate_lin, up_lin, activ, layer_out, d_mlp_low, grad_four = ([] for _ in range(6))
    for i in range(halves):
        gate_lin.append(dot(normed_mlp[i], gate_w))
        up_lin.append(dot(normed_mlp[i], up_w))
        activ.append((gelu(gate_lin[i]) * up_lin[i]).astype(BF16))
        branch = tp_scatter(dot_nt(activ[i], down_w), tp)
        inv = inverse_of(branch)
        layer_out.append(tp_gather((resid[i] + branch * inv * gain_four).astype(BF16), tp))
        d_branch, d_gain = norm_back(branch, inv, gain_four, share_of(cotangent[0], i))
        grad_four.append(d_gain)
        d_mlp_low.append(tp_gather(d_branch.astype(BF16), tp))

    d_gate, d_up, d_resid, d_attn_low, grad_three, grad_two, d_attended = ([] for _ in range(7))
    for i in range(halves):
        d_activ = dot(d_mlp_low[i], down_w)
        bent, slope = gelu_and_slope(gate_lin[i])
        d_gate.append((d_activ * up_lin[i] * slope).astype(BF16))
        d_up.append((d_activ * bent).astype(BF16))
        d_normed = tp_scatter(dot_nt(d_gate[i], gate_w) + dot_nt(d_up[i], up_w), tp)
        d_in, d_gain = norm_back(resid[i], inv_three[i], gain_three, d_normed)
        grad_three.append(d_gain)
        d_resid.append(share_of(cotangent[0], i) + d_in)
        d_branch, d_gain = norm_back(branch_attn[i], inv_two[i], gain_two, d_resid[i])
        grad_two.append(d_gain)
        d_attn_low.append(tp_gather(d_branch.astype(BF16), tp))
        d_attended.append(dot(d_attn_low[i], out_w).astype(BF16))

    def joined(pieces):
        return jnp.concatenate(pieces, axis=0)

    normed_all = joined(normed_mlp)
    grad_down = scatter(wide, dot_tn(joined(d_mlp_low), joined(activ)).astype(BF16), BF16)
    grad_gate = scatter(wide, dot_tn(normed_all, joined(d_gate)).astype(BF16), BF16)
    grad_up = scatter(wide, dot_tn(normed_all, joined(d_up)).astype(BF16), BF16)
    grad_out = scatter(wide, dot_tn(joined(d_attn_low), joined(attended)).astype(BF16), BF16)

    d_queries, d_kv = attend_back(
        info_all, queries, joined(d_attended), kv, joined(inverse_sum), qseg, segs, heads
    )
    d_kv = scatter(near, d_kv, BF16)
    d_q_lin = rotate(
        d_queries.reshape(count, heads, HEAD_DIM) * scale, cosine[:, None], -sine[:, None]
    ).astype(BF16)
    d_key_lin = rotate(d_kv[:, :HEAD_DIM], cosine, -sine).astype(BF16)
    d_lin = jnp.concatenate(
        [d_q_lin.reshape(count, qcols), d_key_lin, d_kv[:, HEAD_DIM:].astype(BF16)], axis=1
    )
    d_normed_attn = dot_nt(d_lin, qkv_w)
    grad_qkv = scatter(wide, dot_tn(normed_attn, d_lin).astype(BF16), BF16)
    grad_one = jnp.sum(d_normed_attn * inputs * inv_one, axis=0)
    grad_tokens = []
    for i in range(halves):
        d_normed = tp_scatter(rows_of(d_normed_attn, i), tp)
        own = share_of(tok, i)
        d_in, unused = norm_back(own, inverse_of(own), gain_one, d_normed)
        grad_tokens.append(tp_gather((d_resid[i] + d_in).astype(BF16), tp))

    grad_gains = jnp.stack([grad_one, sum(grad_two), sum(grad_three), sum(grad_four)])
    grad_gains = grad_gains.reshape(4, group, width // group).transpose(1, 0, 2)
    grad_gains = scatter(wide, grad_gains, F32)[0]
    travelling = grad_gains
    for step in range(1, tp):
        travelling = lax.ppermute(travelling, "tp", tp_pairs(tp))
        grad_gains = grad_gains + travelling

    return (
        joined(layer_out)[None],
        joined(grad_tokens).astype(F32)[None],
        grad_qkv[:, :qcols],
        grad_qkv[:, qcols : qcols + HEAD_DIM],
        grad_qkv[:, qcols + HEAD_DIM :],
        grad_out.T,
        grad_gate,
        grad_up,
        grad_down.T,
        grad_gains[0],
        grad_gains[1],
        grad_gains[2],
        grad_gains[3],
    )


def solution(mesh):
    sizes = dict(mesh.shape)
    split = ("fsdp", "ctx")
    rows, cols = P(split, "tp"), P("tp", split)
    acts, ids = P("fsdp", "ctx", None), P("fsdp", None)
    return jax.shard_map(
        functools.partial(per_device, sizes),
        mesh=mesh,
        in_specs=(acts, rows, rows, rows, cols, rows, rows, cols)
        + (P(split),) * 4
        + (ids, ids, acts),
        out_specs=(acts, acts, rows, rows, rows, cols, rows, rows, cols) + (P(split),) * 4,
        check_vma=False,
    )
```

```python
import functools

import jax
import jax.numpy as jnp
import numpy as np
from jax import lax
from jax.experimental import pallas as pl
from jax.experimental.pallas import tpu as pltpu
from jax.sharding import PartitionSpec as P

HEAD_DIM = 256
BLOCK = 256
EPS = 1e-06
CAP = 50.0
THETA = 10000.0
F32 = jnp.float32
BF16 = jnp.bfloat16


class Ring:
    def __init__(self, sizes, axes):
        self.axes = axes
        outer = sizes[axes[0]] if len(axes) == 2 else 1
        inner = sizes[axes[-1]] // 2
        order = []
        for row in range(outer):
            cols = range(inner) if row % 2 == 0 else reversed(range(inner))
            order += [row * inner + col for col in cols]
        self.order = np.array(order, np.int32)
        self.count = len(order)
        self.place = np.argsort(self.order).astype(np.int32)
        self.sibling = [(i, i ^ 1) for i in range(2 * self.count)]

    def pairs(self, sign):
        out = []
        for pos in range(self.count):
            for core in range(2):
                step = sign if core == 0 else -sign
                there = self.order[(pos + step) % self.count]
                out.append((int(self.order[pos]) * 2 + core, int(there) * 2 + core))
        return out

    def locate(self):
        me = lax.axis_index(self.axes)
        core = me % 2
        pos = jnp.asarray(self.place)[me // 2]
        return pos, core

    def owner(self, pos, core, label):
        step = jnp.where(core == 0, label, -label)
        return jnp.asarray(self.order)[(pos + step) % self.count] * 2 + core

    def swap(self, value):
        return lax.ppermute(value, self.axes, self.sibling)


def after(value, *deps):
    return lax.optimization_barrier((value,) + deps)[0]


def put(buffer, piece, index):
    starts = (index * piece.shape[0],) + (0,) * (buffer.ndim - 1)
    return lax.dynamic_update_slice(buffer, piece, starts)


def gather_steps(ring, shard):
    pos, core = ring.locate()
    whole = jnp.zeros((2 * ring.count * shard.shape[0],) + shard.shape[1:], shard.dtype)
    piece = shard
    for label in range(ring.count):
        if label:
            waits = yield piece
            piece = lax.ppermute(piece, ring.axes, ring.pairs(-1))
            if waits:
                piece = after(piece, *waits)
        other = ring.swap(piece)
        whole = put(whole, piece, ring.owner(pos, core, label))
        whole = put(whole, other, ring.owner(pos, 1 - core, label))
    yield whole


def scatter_steps(ring, value, wire):
    pos, core = ring.locate()
    rows = value.shape[0] // (2 * ring.count)

    def block(kind, label):
        start = ring.owner(pos, kind, label) * rows
        return lax.dynamic_slice_in_dim(value, start, rows).astype(wire)

    labels = range(ring.count)
    other = [ring.swap(block(1 - core, label)) for label in labels]

    def both(label):
        return block(core, label).astype(F32) + other[label].astype(F32)

    total = both(ring.count - 1)
    for label in range(ring.count - 2, -1, -1):
        total = total.astype(wire)
        waits = yield total
        got = lax.ppermute(total, ring.axes, ring.pairs(1))
        if waits:
            got = after(got, *waits)
        total = both(label) + got.astype(F32)
    yield total


def scatter(ring, value, wire):
    return finish(begun(scatter_steps(ring, value, wire)), ring.count - 1)


def tp_pairs(count):
    return [(i, (i + 1) % count) for i in range(count)]


def tp_scatter(part, count):
    here = lax.axis_index("tp")
    rows = part.shape[0] // count

    def chunk(back):
        return lax.dynamic_slice_in_dim(part, ((here - back) % count) * rows, rows)

    total = chunk(1).astype(BF16)
    for step in range(1, count):
        waits = yield total
        got = lax.ppermute(total, "tp", tp_pairs(count))
        if waits:
            got = after(got, *waits)
        total = chunk(step + 1).astype(F32) + got.astype(F32)
        if step + 1 < count:
            total = total.astype(BF16)
    yield total


def tp_gather(own, count, kind=BF16):
    here = lax.axis_index("tp")
    axis = own.ndim - 2
    rows = own.shape[axis]
    shape = own.shape[:axis] + (count * rows,) + own.shape[axis + 1 :]

    def place(whole, piece, index):
        return lax.dynamic_update_slice_in_dim(whole, piece.astype(kind), index * rows, axis)

    whole = place(jnp.zeros(shape, kind), own, here)
    piece = own
    for step in range(1, count):
        waits = yield piece
        piece = lax.ppermute(piece, "tp", tp_pairs(count))
        if waits:
            piece = after(piece, *waits)
        whole = place(whole, piece, (here - step) % count)
    yield whole


def step(steps, *waits):
    return steps.send(waits)


def begun(steps):
    next(steps)
    return steps


def finish(steps, count):
    for _ in range(count):
        last = step(steps)
    return last


def inverse_of(values):
    return lax.rsqrt(jnp.mean(values * values, axis=-1, keepdims=True) + EPS)


def norm_back(values, inverse, gain, upstream):
    scaled = upstream * gain
    d_values = inverse * scaled - values * (
        inverse * inverse * inverse * jnp.mean(scaled * values, axis=-1, keepdims=True)
    )
    return d_values, jnp.sum(upstream * values * inverse, axis=0)


def rotate(values, cosine, sine):
    half = values.shape[-1] // 2
    first, second = values[..., :half], values[..., half:]
    return jnp.concatenate(
        [first * cosine - second * sine, second * cosine + first * sine], axis=-1
    )


def dot(left, right):
    return jnp.dot(left, right, preferred_element_type=F32)


def dot_nt(left, right):
    return lax.dot_general(left, right, (((1,), (1,)), ((), ())), preferred_element_type=F32)


def dot_tn(left, right):
    return lax.dot_general(left, right, (((0,), (0,)), ((), ())), preferred_element_type=F32)


GELU_A = 0.7978845608028654
GELU_B = 0.044715


def gelu(gate):
    return 0.5 * gate * (1.0 + jnp.tanh(GELU_A * (gate + GELU_B * gate * gate * gate)))


def gelu_and_slope(gate):
    square = gate * gate
    bent = jnp.tanh(GELU_A * (gate + GELU_B * gate * square))
    half = 0.5 * (1.0 + bent)
    slope = half + 0.5 * gate * (1.0 - bent * bent) * GELU_A * (1.0 + 3.0 * GELU_B * square)
    return gate * half, slope


def spec(shape, where):
    return pl.BlockSpec(shape, where)


TILE = 768


def call(body, grid, in_specs, out_specs, out_shape, flops, moved, name, limit=44):
    return pl.pallas_call(
        body,
        grid=(grid,),
        in_specs=in_specs,
        out_specs=out_specs,
        out_shape=out_shape,
        compiler_params=pltpu.CompilerParams(
            dimension_semantics=("arbitrary",), vmem_limit_bytes=limit << 20
        ),
        cost_estimate=pl.CostEstimate(flops=flops, bytes_accessed=moved, transcendentals=0),
        name=name,
    )


def held_kernel(*refs):
    pass


def held(value, *deps):
    return pl.pallas_call(
        held_kernel,
        in_specs=[pl.BlockSpec(memory_space=pl.ANY)] * (1 + len(deps)),
        out_specs=pl.BlockSpec(memory_space=pl.ANY),
        out_shape=jax.ShapeDtypeStruct(value.shape, value.dtype),
        input_output_aliases={0: 0},
        compiler_params=pltpu.CompilerParams(has_side_effects=True),
        name="held",
    )(value, *deps)


def gate_up_kernel(x_ref, gate_ref, up_ref, gate_out, up_out, activ_out):
    gate = dot(x_ref[...], gate_ref[...])
    up = dot(x_ref[...], up_ref[...])
    gate_out[...] = gate
    up_out[...] = up
    activ_out[...] = (gelu(gate) * up).astype(BF16)


def gate_up(x, weights):
    rows, depth = x.shape
    units = weights.shape[1] // 2
    tiles = units // TILE
    tile = spec((rows, TILE), lambda j: (0, j))
    return call(
        gate_up_kernel,
        tiles,
        [
            spec((rows, depth), lambda j: (0, 0)),
            spec((depth, TILE), lambda j: (0, j)),
            spec((depth, TILE), lambda j: (0, j + tiles)),
        ],
        (tile, tile, tile),
        tuple(jax.ShapeDtypeStruct((rows, units), kind) for kind in (F32, F32, BF16)),
        4 * rows * depth * units,
        4 * depth * units + 12 * rows * units,
        "gate_up",
    )(x, weights, weights)


def down_kernel(x_ref, w_ref, out_ref):
    out_ref[...] = dot_nt(x_ref[...], w_ref[...]).astype(out_ref.dtype)


def down(x, weights):
    rows, units = x.shape
    width = weights.shape[0]
    return call(
        down_kernel,
        width // TILE,
        [spec((rows, units), lambda j: (0, 0)), spec((TILE, units), lambda j: (j, 0))],
        spec((rows, TILE), lambda j: (0, j)),
        jax.ShapeDtypeStruct((rows, width), BF16),
        2 * rows * width * units,
        2 * width * units,
        "down",
    )(x, weights)


def d_activ_kernel(x_ref, w_ref, gate_ref, up_ref, d_gate_ref, d_up_ref):
    d_activ = dot(x_ref[...], w_ref[...])
    bent, slope = gelu_and_slope(gate_ref[...])
    d_gate_ref[...] = (d_activ * up_ref[...] * slope).astype(BF16)
    d_up_ref[...] = (d_activ * bent).astype(BF16)


def d_gate_up(x, weights, gate_lin, up_lin):
    rows, width = x.shape
    units = weights.shape[1]
    tile = spec((rows, TILE), lambda j: (0, j))
    return call(
        d_activ_kernel,
        units // TILE,
        [
            spec((rows, width), lambda j: (0, 0)),
            spec((width, TILE), lambda j: (0, j)),
            tile,
            tile,
        ],
        (tile, tile),
        tuple(jax.ShapeDtypeStruct((rows, units), BF16) for _ in range(2)),
        2 * rows * width * units,
        2 * width * units + 12 * rows * units,
        "d_gate_up",
    )(x, weights, gate_lin, up_lin)


def d_normed_kernel(a_ref, b_ref, wa_ref, wb_ref, out_ref):
    total = dot_nt(a_ref[...], wa_ref[...]) + dot_nt(b_ref[...], wb_ref[...])
    out_ref[...] = total.astype(out_ref.dtype)


def d_normed_of(d_gate, d_up, weights):
    rows, units = d_gate.shape
    width = weights.shape[0]
    whole = spec((rows, units), lambda j: (0, 0))
    return call(
        d_normed_kernel,
        width // TILE,
        [
            whole,
            whole,
            spec((TILE, units), lambda j: (j, 0)),
            spec((TILE, units), lambda j: (j, 1)),
        ],
        spec((rows, TILE), lambda j: (0, j)),
        jax.ShapeDtypeStruct((rows, width), BF16),
        4 * rows * width * units,
        4 * width * units,
        "d_normed",
    )(d_gate, d_up, weights, weights)


def outer_kernel(a_ref, b_ref, out_ref):
    out_ref[...] = dot_tn(a_ref[...], b_ref[...]).astype(out_ref.dtype)


def outer(left, right, name):
    rows, width = left.shape
    units = right.shape[1]
    return call(
        outer_kernel,
        width // TILE,
        [spec((rows, TILE), lambda j: (0, j)), spec((rows, units), lambda j: (0, 0))],
        spec((TILE, units), lambda j: (j, 0)),
        jax.ShapeDtypeStruct((width, units), BF16),
        2 * rows * width * units,
        2 * width * units,
        name,
    )(left, right)


def outer_pair_kernel(a_ref, b_ref, c_ref, *rest):
    out_ref = rest[-1]
    units = b_ref.shape[1]
    out_ref[:, :units] = dot_tn(a_ref[...], b_ref[...]).astype(out_ref.dtype)
    out_ref[:, units:] = dot_tn(a_ref[...], c_ref[...]).astype(out_ref.dtype)


def outer_pair(left, right, other, begun, name):
    rows, width = left.shape
    units = right.shape[1]
    whole = spec((rows, units), lambda j: (0, 0))
    tiles = width // TILE
    most = tiles - tiles // 2
    start, grid = (0, most) if begun is None else (most, tiles - most)
    more = [] if begun is None else [begun]
    return pl.pallas_call(
        outer_pair_kernel,
        grid=(grid,),
        in_specs=[spec((rows, TILE), lambda j: (0, j + start)), whole, whole]
        + [pl.BlockSpec(memory_space=pl.ANY)] * len(more),
        out_specs=spec((TILE, 2 * units), lambda j: (j + start, 0)),
        out_shape=jax.ShapeDtypeStruct((width, 2 * units), BF16),
        input_output_aliases={3: 0} if more else {},
        compiler_params=pltpu.CompilerParams(
            dimension_semantics=("arbitrary",), vmem_limit_bytes=44 << 20
        ),
        cost_estimate=pl.CostEstimate(
            flops=4 * rows * grid * TILE * units,
            bytes_accessed=4 * grid * TILE * units,
            transcendentals=0,
        ),
        name=name,
    )(left, right, other, *more)


def outer_two_kernel(a_ref, b_ref, c_ref, d_ref, more_ref, out_ref):
    units = b_ref.shape[1]
    both = units + d_ref.shape[1]
    out_ref[:, :units] = dot_tn(a_ref[...], b_ref[...]).astype(out_ref.dtype)
    out_ref[:, units:both] = dot_tn(c_ref[...], d_ref[...]).astype(out_ref.dtype)
    out_ref[:, both:] = more_ref[...].astype(out_ref.dtype)


def outer_two(left, right, left_b, right_b, extra, name):
    rows, width = left.shape
    units, more = right.shape[1], right_b.shape[1]
    side = spec((rows, TILE), lambda j: (0, j))
    return call(
        outer_two_kernel,
        width // TILE,
        [
            side,
            spec((rows, units), lambda j: (0, 0)),
            side,
            spec((rows, more), lambda j: (0, 0)),
            spec((TILE, extra.shape[1]), lambda j: (j, 0)),
        ],
        spec((TILE, units + more + extra.shape[1]), lambda j: (j, 0)),
        jax.ShapeDtypeStruct((width, units + more + extra.shape[1]), BF16),
        2 * rows * width * (units + more),
        2 * width * (units + more),
        name,
    )(left, right, left_b, right_b, extra)


def stack_heads(ref, rows, first, count):
    return jnp.concatenate(
        [ref[rows, pl.ds((first + h) * HEAD_DIM, HEAD_DIM)] for h in range(count)], axis=0
    )


def attend_kernel(heads, info, q_ref, kv_ref, qseg_ref, kseg_ref, out_ref, inv_ref, p_ref):
    low, high = info[0], info[1]
    rows = heads * BLOCK
    every = pl.ds(0, BLOCK)
    query = stack_heads(q_ref, every, 0, heads)
    qseg = jnp.concatenate([qseg_ref[...]] * heads, axis=0)

    def first(j, acc):
        start = pl.multiple_of(info[2 + j] * BLOCK, BLOCK)
        scores = dot_nt(query, kv_ref[pl.ds(start, BLOCK), pl.ds(0, HEAD_DIM)])
        weight = jnp.exp(CAP * jnp.tanh(scores * (1.0 / CAP)))
        weight = jnp.where(qseg == kseg_ref[pl.ds(j, 1), :], weight, 0.0)
        p_ref[j] = weight
        return acc + weight[:, :128] + weight[:, 128:]

    acc = lax.fori_loop(low, high + 1, first, jnp.zeros((rows, 128), F32))
    inverse = 1.0 / jnp.sum(acc, axis=1, keepdims=True)
    inv_ref[...] = inverse

    def second(j, total):
        start = pl.multiple_of(info[2 + j] * BLOCK, BLOCK)
        low_probs = (p_ref[j] * inverse).astype(BF16)
        return total + dot(low_probs, kv_ref[pl.ds(start, BLOCK), pl.ds(HEAD_DIM, HEAD_DIM)])

    total = lax.fori_loop(low, high + 1, second, jnp.zeros((rows, HEAD_DIM), F32))
    for h in range(heads):
        out_ref[:, pl.ds(h * HEAD_DIM, HEAD_DIM)] = total[h * BLOCK : (h + 1) * BLOCK].astype(BF16)


def vmem():
    return pl.BlockSpec(memory_space=pltpu.VMEM)


def attend(info, queries, kv, qseg, kseg, heads):
    blocks = kseg.shape[0]
    return pl.pallas_call(
        functools.partial(attend_kernel, heads),
        out_shape=(
            jax.ShapeDtypeStruct((BLOCK, heads * HEAD_DIM), BF16),
            jax.ShapeDtypeStruct((heads * BLOCK, 1), F32),
        ),
        in_specs=[pl.BlockSpec(memory_space=pltpu.SMEM)] + [vmem()] * 4,
        out_specs=(vmem(), vmem()),
        scratch_shapes=[pltpu.VMEM((blocks, heads * BLOCK, BLOCK), F32)],
        compiler_params=pltpu.CompilerParams(vmem_limit_bytes=(16 if blocks <= 8 else 48) << 20),
        cost_estimate=pl.CostEstimate(
            flops=3 * heads * BLOCK * blocks * BLOCK * HEAD_DIM,
            bytes_accessed=4 << 20,
            transcendentals=heads * BLOCK * blocks * BLOCK,
        ),
        name="attend",
    )(info, queries, kv, qseg, kseg)


def attend_back_kernel(
    heads, each, info, q_ref, do_ref, kv_ref, inv_ref, qseg_ref, kseg_ref, dq_ref, dkv_ref,
    p_ref, g_ref, dp_ref,
):
    blocks_q = q_ref.shape[0] // BLOCK
    dkv_ref[...] = jnp.zeros(dkv_ref.shape, F32)
    keys = pl.ds(0, HEAD_DIM)
    vals = pl.ds(HEAD_DIM, HEAD_DIM)
    for i in range(blocks_q):
        low, high = info[2 * i], info[2 * i + 1]
        qrows = pl.ds(i * BLOCK, BLOCK)
        qseg = jnp.concatenate([qseg_ref[qrows, :]] * each, axis=0)
        for h in range(0, heads, each):
            query = stack_heads(q_ref, qrows, h, each)
            d_out = stack_heads(do_ref, qrows, h, each)
            inverse = inv_ref[pl.ds((i * heads + h) * BLOCK, each * BLOCK), :]

            def first(j, acc, query=query, d_out=d_out, inverse=inverse, qseg=qseg):
                start = pl.multiple_of(info[2 * blocks_q + j] * BLOCK, BLOCK)
                place = pl.ds(start, BLOCK)
                bent = jnp.tanh(dot_nt(query, kv_ref[place, keys]) * (1.0 / CAP))
                probs = jnp.exp(CAP * bent) * inverse
                probs = jnp.where(qseg == kseg_ref[pl.ds(j, 1), :], probs, 0.0)
                d_probs = dot_nt(d_out, kv_ref[place, vals])
                p_ref[j] = probs.astype(BF16)
                g_ref[j] = probs * (1.0 - bent * bent)
                dp_ref[j] = d_probs
                both = probs * d_probs
                return acc + both[:, :128] + both[:, 128:]

            acc = lax.fori_loop(low, high + 1, first, jnp.zeros((each * BLOCK, 128), F32))
            inner = jnp.sum(acc, axis=1, keepdims=True)

            def second(j, total, query=query, d_out=d_out, inner=inner):
                start = pl.multiple_of(info[2 * blocks_q + j] * BLOCK, BLOCK)
                place = pl.ds(start, BLOCK)
                d_scores = (g_ref[j] * (dp_ref[j] - inner)).astype(BF16)
                dkv_ref[place, keys] += dot_tn(d_scores, query)
                dkv_ref[place, vals] += dot_tn(p_ref[j], d_out)
                return total + dot(d_scores, kv_ref[place, keys])

            total = lax.fori_loop(
                low, high + 1, second, jnp.zeros((each * BLOCK, HEAD_DIM), F32)
            )
            for n in range(each):
                dq_ref[qrows, pl.ds((h + n) * HEAD_DIM, HEAD_DIM)] = total[
                    n * BLOCK : (n + 1) * BLOCK
                ]


def attend_back(info, queries, d_out, kv, inverse, qseg, kseg, heads):
    blocks = kseg.shape[0]
    each = heads if blocks <= 8 else 1
    tile = (blocks, each * BLOCK, BLOCK)
    return pl.pallas_call(
        functools.partial(attend_back_kernel, heads, each),
        out_shape=(
            jax.ShapeDtypeStruct(queries.shape, F32),
            jax.ShapeDtypeStruct(kv.shape, F32),
        ),
        in_specs=[pl.BlockSpec(memory_space=pltpu.SMEM)] + [vmem()] * 6,
        out_specs=(vmem(), vmem()),
        scratch_shapes=[pltpu.VMEM(tile, BF16), pltpu.VMEM(tile, F32), pltpu.VMEM(tile, F32)],
        compiler_params=pltpu.CompilerParams(vmem_limit_bytes=(26 if blocks <= 8 else 56) << 20),
        cost_estimate=pl.CostEstimate(
            flops=11 * heads * BLOCK * blocks * BLOCK * HEAD_DIM,
            bytes_accessed=10 << 20,
            transcendentals=2 * heads * BLOCK * blocks * BLOCK,
        ),
        name="attend_back",
    )(info, queries, d_out, kv, inverse, qseg, kseg)


def per_device(
    sizes,
    tokens,
    q_weight,
    key_weight,
    value_weight,
    out_weight,
    gate_weight,
    up_weight,
    down_weight,
    gain_attn_in,
    gain_attn_out,
    gain_mlp_in,
    gain_mlp_out,
    segment_ids,
    block_order,
    cotangent,
):
    tp = sizes["tp"]
    wide = Ring(sizes, ("fsdp", "ctx"))
    near = Ring(sizes, ("ctx",))
    group = 2 * wide.count
    here = lax.axis_index("tp")
    tok = tokens[0]
    count, width = tok.shape
    halves = count // BLOCK
    share = BLOCK // tp
    heads = q_weight.shape[1] // HEAD_DIM
    qcols = q_weight.shape[1]

    split = ("fsdp", "ctx")
    gains_own = jnp.stack([gain_attn_in, gain_attn_out, gain_mlp_in, gain_mlp_out])
    gains_own = jnp.pad(gains_own, ((0, 124), (0, 0))).T
    attn_own = jnp.concatenate(
        [q_weight, key_weight, value_weight, out_weight.T, gains_own], axis=1
    )
    attn_w = lax.all_gather(attn_own, split, axis=0, tiled=True)
    gu_own = jnp.concatenate([gate_weight, after(up_weight, attn_own)], axis=1)
    gu_w = lax.all_gather(after(gu_own, attn_w), split, axis=0, tiled=True)
    down_own = after(down_weight, gu_own).T
    lin_cols = qcols + 2 * HEAD_DIM
    out_cols = lin_cols + out_weight.shape[0]
    qkv_w, out_w = attn_w[:, :lin_cols], attn_w[:, lin_cols:out_cols]
    gains = attn_w[:, out_cols:].T.astype(F32)
    gain_one, gain_two, gain_three, gain_four = (gains[i] for i in range(4))

    order = block_order[0]
    blocks = order.shape[0]
    stored = jnp.argsort(order).astype(jnp.int32)
    segs = segment_ids[0].reshape(blocks, BLOCK)
    first_block = lax.axis_index("ctx") * halves
    high = lax.dynamic_slice_in_dim(order, first_block, halves)
    qsegs = segs[high]
    low = jnp.sum((segs[None, :, -1] < qsegs[:, :1]).astype(jnp.int32), axis=1)
    bounds = jnp.stack([low, high], axis=1).astype(jnp.int32)
    infos = [jnp.concatenate([bounds[i], stored]) for i in range(halves)]
    info_all = jnp.concatenate([bounds.reshape(-1), stored])
    qseg = qsegs.reshape(count, 1)

    spot = (high[:, None] * BLOCK + jnp.arange(BLOCK, dtype=jnp.int32)[None]).reshape(-1)
    half_dim = HEAD_DIM // 2
    freqs = THETA ** (-jnp.arange(half_dim, dtype=F32) * 2.0 / HEAD_DIM)
    angles = spot.astype(F32)[:, None] * freqs[None, :]
    cosine, sine = jnp.cos(angles), jnp.sin(angles)
    scale = HEAD_DIM**-0.5

    inputs = tok.astype(F32)
    inv_one = inverse_of(inputs)
    normed_attn = (inputs * inv_one * gain_one).astype(BF16)
    lin = dot(normed_attn, qkv_w)
    q_lin = lin[:, :qcols].reshape(count, heads, HEAD_DIM)
    queries = (rotate(q_lin, cosine[:, None], sine[:, None]) * scale).astype(BF16)
    queries = queries.reshape(count, qcols)
    keys = rotate(lin[:, qcols : qcols + HEAD_DIM], cosine, sine).astype(BF16)
    values = lin[:, qcols + HEAD_DIM :].astype(BF16)
    kv_own = jnp.concatenate([keys, values], axis=1)
    kv_move = begun(gather_steps(near, kv_own))
    for _ in range(near.count - 1):
        kv = step(kv_move, queries, qseg, *infos)
    down_move = gather_steps(wide, after(down_own, attn_w))
    passing = next(down_move)
    down_left = wide.count - 1

    def pass_down(*waits):
        nonlocal passing, down_left
        if down_left:
            passing, down_left = step(down_move, *waits), down_left - 1

    pass_down(kv)

    def rows_of(array, i):
        return lax.slice_in_dim(array, i * BLOCK, (i + 1) * BLOCK)

    def share_of(array, i):
        return lax.dynamic_slice_in_dim(array, i * BLOCK + here * share, share).astype(F32)

    def joined(pieces):
        return jnp.concatenate(pieces, axis=0)

    hops = tp - 1
    both = range(halves)

    def all_steps(parts):
        for _ in range(hops):
            last = [step(part) for part in parts]
        return last

    attended, inverse_sum, sums = [], [], []
    for i in both:
        out, inv = attend(infos[i], rows_of(queries, i), kv, rows_of(qseg, i), segs, heads)
        attended.append(out)
        inverse_sum.append(inv)
        sums.append(tp_scatter(dot_nt(out, out_w).astype(BF16), tp))
        next(sums[i])
    for n in range(hops):
        branch_attn = [step(part) for part in sums]
        if n == 1:
            pass_down(*branch_attn)
    inv_two = [inverse_of(branch) for branch in branch_attn]
    resid = [share_of(tok, i) + branch_attn[i] * inv_two[i] * gain_two for i in both]
    inv_three = [inverse_of(value) for value in resid]
    moves = [tp_gather((resid[i] * inv_three[i] * gain_three).astype(BF16), tp) for i in both]
    for move in moves:
        next(move)
    for n in range(hops - 1):
        sent = [step(move) for move in moves]
        if n == 0:
            pass_down(*sent)
    first = step(moves[0])
    while down_left:
        pass_down()
    down_w = passing

    gate_lin, up_lin, activ = [None] * halves, [None] * halves, [None] * halves
    gate_lin[0], up_lin[0], activ[0] = gate_up(after(first, sent[-1]), gu_w)
    normed_mlp = [first] + [step(move, activ[0]) for move in moves[1:]]
    sums = [tp_scatter(down(activ[0], down_w), tp)]
    sent = next(sums[0])
    gate_lin[1], up_lin[1], activ[1] = gate_up(after(normed_mlp[1], sent), gu_w)
    sent = step(sums[0], activ[1])
    part = down(after(activ[1], sent), down_w)
    sums.append(tp_scatter(part, tp))
    next(sums[1])
    sent = step(sums[0], part)

    layer_own, grad_four, moves = [], [], []

    def middle(i, branch):
        inv = inverse_of(branch)
        layer_own.append((resid[i] + branch * inv * gain_four).astype(BF16))
        d_branch, d_gain = norm_back(branch, inv, gain_four, share_of(cotangent[0], i))
        grad_four.append(d_gain)
        moves.append(tp_gather(d_branch.astype(BF16), tp))
        return next(moves[i])

    step(sums[1])
    middle(0, step(sums[0]))
    step(sums[1])
    step(moves[0])
    middle(1, step(sums[1]))
    step(moves[0])
    step(moves[1])
    first = step(moves[0])
    sent = step(moves[1])
    layer_move = begun(tp_gather(after(jnp.stack(layer_own), first), tp))

    d_gate, d_up = [None] * halves, [None] * halves
    d_gate[0], d_up[0] = d_gate_up(after(first, sent), down_w, gate_lin[0], up_lin[0])
    d_mlp_low = [first, step(moves[1], d_gate[0])]
    grad_down = outer(joined(d_mlp_low), joined(activ), "grad_down")
    sent_layer = step(layer_move, grad_down)
    part = d_normed_of(after(d_gate[0], grad_down, sent_layer), d_up[0], gu_w)
    sums = [tp_scatter(part, tp)]
    sent = next(sums[0])
    d_gate[1], d_up[1] = d_gate_up(after(d_mlp_low[1], sent), down_w, gate_lin[1], up_lin[1])
    sent = step(sums[0], d_gate[1])
    sent_layer = step(layer_move, sent)
    part = d_normed_of(after(d_gate[1], sent, sent_layer), d_up[1], gu_w)
    sums.append(tp_scatter(part, tp))
    next(sums[1])
    d_resid, grad_three, grad_two, moves = [], [], [], []

    def middle_back(i, part):
        d_in, d_gain = norm_back(resid[i], inv_three[i], gain_three, part)
        grad_three.append(d_gain)
        d_resid.append(share_of(cotangent[0], i) + d_in)
        d_branch, d_gain = norm_back(branch_attn[i], inv_two[i], gain_two, d_resid[i])
        grad_two.append(d_gain)
        moves.append(tp_gather(d_branch.astype(BF16), tp))
        return next(moves[i])

    step(sums[0], part)
    sent = middle_back(0, step(sums[0]))
    layer_out = step(layer_move, part)
    normed_all = joined(normed_mlp)
    d_pair = joined(d_gate), joined(d_up)
    grad_gu = outer_pair(after(normed_all, sent, layer_out), *d_pair, None, "grad_gate_up")
    mark = grad_gu[:8, :128]
    sent = step(sums[1], mark), step(moves[0], mark)
    grad_gu = outer_pair(after(normed_all, *sent), *d_pair, grad_gu, "grad_gate_up_more")
    mark = grad_gu[-8:, :128]
    step(sums[1], mark), step(moves[0], mark)
    grad_down = lax.psum_scatter(grad_down, split, scatter_dimension=0, tiled=True)
    sent = middle_back(1, step(sums[1]))
    grad_gu = held(grad_gu, grad_down, sent)
    grad_gu = lax.psum_scatter(grad_gu, split, scatter_dimension=0, tiled=True)
    grad_down = grad_down.astype(F32)
    first = step(moves[0])
    d_attn_low = [first, finish(moves[1], hops)]

    d_attn_all = joined(d_attn_low)
    d_attended = dot(d_attn_all, out_w).astype(BF16)
    d_queries, d_kv = attend_back(
        info_all, queries, d_attended, kv, joined(inverse_sum), qseg, segs, heads
    )
    d_q_lin = rotate(
        d_queries.reshape(count, heads, HEAD_DIM) * scale, cosine[:, None], -sine[:, None]
    ).astype(BF16)
    d_q_lin = d_q_lin.reshape(count, qcols)
    from_q = dot_nt(d_q_lin, qkv_w[:, :qcols])
    d_kv = scatter(near, d_kv, BF16)
    d_key_lin = rotate(d_kv[:, :HEAD_DIM], cosine, -sine).astype(BF16)
    d_kv_lin = jnp.concatenate([d_key_lin, d_kv[:, HEAD_DIM:].astype(BF16)], axis=1)
    d_normed_attn = from_q + dot_nt(d_kv_lin, qkv_w[:, qcols:])
    d_normed_low = d_normed_attn.astype(BF16)
    sums = [tp_scatter(rows_of(d_normed_low, i), tp) for i in both]
    sent = [next(part) for part in sums]
    grad_one = jnp.sum(after(d_normed_attn, *sent) * inputs * inv_one, axis=0)
    grad_gains = jnp.stack([grad_one, sum(grad_two), sum(grad_three), sum(grad_four)])
    grad_gains = jnp.pad(grad_gains, ((0, 124), (0, 0))).T
    d_lin = jnp.concatenate([d_q_lin, d_kv_lin], axis=1)
    grad_attn = outer_two(
        normed_attn, d_lin, d_attn_all, joined(attended), grad_gains, "grad_attn"
    )
    for _ in range(hops):
        sent = [step(part) for part in sums]
    moves = []
    for i in both:
        own = share_of(tok, i)
        d_in, unused = norm_back(own, inverse_of(own), gain_one, sent[i])
        moves.append(begun(tp_gather((d_resid[i] + d_in).astype(BF16), tp, F32)))
        sent[i] = step(moves[i])
    grad_attn = held(grad_attn, grad_gu, *sent)
    grad_gu = grad_gu.astype(F32)
    grad_attn = lax.psum_scatter(grad_attn, split, scatter_dimension=0, tiled=True).astype(F32)
    for _ in range(hops - 1):
        grad_tokens = [step(move) for move in moves]
    grad_gains = grad_attn[:, out_cols:]
    bit = 1
    while bit < tp:
        swap = [(i, i ^ bit) for i in range(tp)]
        grad_gains = grad_gains + lax.ppermute(grad_gains, "tp", swap)
        bit *= 2
    grad_qkv, grad_out = grad_attn[:, :lin_cols], grad_attn[:, lin_cols:out_cols]
    grad_gains = grad_gains.T

    return (
        layer_out.reshape(1, count, width),
        joined(grad_tokens)[None],
        grad_qkv[:, :qcols],
        grad_qkv[:, qcols : qcols + HEAD_DIM],
        grad_qkv[:, qcols + HEAD_DIM :],
        grad_out.T,
        grad_gu[:, : gate_weight.shape[1]],
        grad_gu[:, gate_weight.shape[1] :],
        grad_down.T,
        grad_gains[0],
        grad_gains[1],
        grad_gains[2],
        grad_gains[3],
    )


def solution(mesh):
    sizes = dict(mesh.shape)
    split = ("fsdp", "ctx")
    rows, cols = P(split, "tp"), P("tp", split)
    acts, ids = P("fsdp", "ctx", None), P("fsdp", None)
    return jax.shard_map(
        functools.partial(per_device, sizes),
        mesh=mesh,
        in_specs=(acts, rows, rows, rows, cols, rows, rows, cols)
        + (P(split),) * 4
        + (ids, ids, acts),
        out_specs=(acts, acts, rows, rows, rows, cols, rows, rows, cols) + (P(split),) * 4,
        check_vma=False,
    )
```

```python
import functools

import jax
import jax.numpy as jnp
import numpy as np
from jax import lax
from jax.experimental import pallas as pl
from jax.experimental.pallas import tpu as pltpu
from jax.sharding import PartitionSpec as P

HEAD_DIM = 256
BLOCK = 256
EPS = 1e-06
CAP = 50.0
THETA = 10000.0
F32 = jnp.float32
BF16 = jnp.bfloat16


class Ring:
    def __init__(self, sizes, axes):
        self.axes = axes
        outer = sizes[axes[0]] if len(axes) == 2 else 1
        inner = sizes[axes[-1]] // 2
        order = []
        for row in range(outer):
            cols = range(inner) if row % 2 == 0 else reversed(range(inner))
            order += [row * inner + col for col in cols]
        self.order = np.array(order, np.int32)
        self.count = len(order)
        self.place = np.argsort(self.order).astype(np.int32)
        self.sibling = [(i, i ^ 1) for i in range(2 * self.count)]

    def pairs(self, sign):
        out = []
        for pos in range(self.count):
            for core in range(2):
                step = sign if core == 0 else -sign
                there = self.order[(pos + step) % self.count]
                out.append((int(self.order[pos]) * 2 + core, int(there) * 2 + core))
        return out

    def locate(self):
        me = lax.axis_index(self.axes)
        core = me % 2
        pos = jnp.asarray(self.place)[me // 2]
        return pos, core

    def owner(self, pos, core, label):
        step = jnp.where(core == 0, label, -label)
        return jnp.asarray(self.order)[(pos + step) % self.count] * 2 + core

    def swap(self, value):
        return lax.ppermute(value, self.axes, self.sibling)


def after(value, *deps):
    return lax.optimization_barrier((value,) + deps)[0]


def put(buffer, piece, index):
    starts = (index * piece.shape[0],) + (0,) * (buffer.ndim - 1)
    return lax.dynamic_update_slice(buffer, piece, starts)


def blank_kernel(ref):
    pass


def blank(shape, kind):
    return pl.pallas_call(
        blank_kernel,
        out_specs=pl.BlockSpec(memory_space=pl.ANY),
        out_shape=jax.ShapeDtypeStruct(shape, kind),
        compiler_params=pltpu.CompilerParams(has_side_effects=True),
        name="blank",
    )()


def put_two_kernel(spots, whole_ref, one_ref, two_ref, out_ref, sems):
    rows = one_ref.shape[0]
    copies = []
    for n, ref in enumerate((one_ref, two_ref)):
        start = pl.multiple_of(spots[n] * rows, 16)
        copies.append(pltpu.make_async_copy(ref, out_ref.at[pl.ds(start, rows)], sems.at[n]))
    for copy in copies:
        copy.start()
    for copy in copies:
        copy.wait()


def put_two(whole, one, spot, two, other_spot):
    if one.shape[0] % 16:
        return put(put(whole, one, spot), two, other_spot)
    anywhere = pl.BlockSpec(memory_space=pl.ANY)
    return pl.pallas_call(
        put_two_kernel,
        in_specs=[pl.BlockSpec(memory_space=pltpu.SMEM), anywhere, vmem(), vmem()],
        out_specs=anywhere,
        out_shape=jax.ShapeDtypeStruct(whole.shape, whole.dtype),
        scratch_shapes=[pltpu.SemaphoreType.DMA((2,))],
        input_output_aliases={1: 0},
        cost_estimate=pl.CostEstimate(flops=0, bytes_accessed=8 * one.size, transcendentals=0),
        name="put_two",
    )(jnp.stack([spot, other_spot]).astype(jnp.int32), whole, one, two)


def gather_steps(ring, shard, first=None):
    pos, core = ring.locate()
    whole = blank((2 * ring.count * shard.shape[0],) + shard.shape[1:], shard.dtype)
    piece = shard
    for label in range(ring.count):
        if label:
            if label == 1 and first is not None:
                piece = after(piece, first)
            waits = yield piece
            piece = lax.ppermute(piece, ring.axes, ring.pairs(-1))
            if waits:
                piece = after(piece, *waits)
        other = ring.swap(piece)
        spots = ring.owner(pos, core, label), ring.owner(pos, 1 - core, label)
        if first is None:
            whole = put_two(whole, piece, spots[0], other, spots[1])
        else:
            whole = put(put(whole, piece, spots[0]), other, spots[1])
    yield whole


def scatter_steps(ring, value, wire):
    pos, core = ring.locate()
    rows = value.shape[0] // (2 * ring.count)

    def block(kind, label):
        start = ring.owner(pos, kind, label) * rows
        return lax.dynamic_slice_in_dim(value, start, rows).astype(wire)

    labels = range(ring.count)
    other = [ring.swap(block(1 - core, label)) for label in labels]

    def both(label):
        return block(core, label).astype(F32) + other[label].astype(F32)

    total = both(ring.count - 1)
    for label in range(ring.count - 2, -1, -1):
        total = total.astype(wire)
        waits = yield total
        got = lax.ppermute(total, ring.axes, ring.pairs(1))
        if waits:
            got = after(got, *waits)
        total = both(label) + got.astype(F32)
    yield total


def scatter(ring, value, wire):
    return finish(begun(scatter_steps(ring, value, wire)), ring.count - 1)


def tp_pairs(count):
    return [(i, (i + 1) % count) for i in range(count)]


def tp_scatter(part, count):
    here = lax.axis_index("tp")
    rows = part.shape[0] // count

    def chunk(back):
        return lax.dynamic_slice_in_dim(part, ((here - back) % count) * rows, rows)

    total = chunk(1).astype(BF16)
    for step in range(1, count):
        waits = yield total
        got = lax.ppermute(total, "tp", tp_pairs(count))
        if waits:
            got = after(got, *waits)
        total = chunk(step + 1).astype(F32) + got.astype(F32)
        if step + 1 < count:
            total = total.astype(BF16)
    yield total


def tp_gather(own, count, kind=BF16):
    here = lax.axis_index("tp")
    axis = own.ndim - 2
    rows = own.shape[axis]
    shape = own.shape[:axis] + (count * rows,) + own.shape[axis + 1 :]

    def place(whole, piece, index):
        return lax.dynamic_update_slice_in_dim(whole, piece.astype(kind), index * rows, axis)

    whole = place(jnp.zeros(shape, kind), own, here)
    piece = own
    for step in range(1, count):
        waits = yield piece
        piece = lax.ppermute(piece, "tp", tp_pairs(count))
        if waits:
            piece = after(piece, *waits)
        whole = place(whole, piece, (here - step) % count)
    yield whole


def step(steps, *waits):
    return steps.send(waits)


def begun(steps):
    next(steps)
    return steps


def finish(steps, count):
    for _ in range(count):
        last = step(steps)
    return last


def inverse_of(values):
    return lax.rsqrt(jnp.mean(values * values, axis=-1, keepdims=True) + EPS)


def norm_back(values, inverse, gain, upstream):
    scaled = upstream * gain
    d_values = inverse * scaled - values * (
        inverse * inverse * inverse * jnp.mean(scaled * values, axis=-1, keepdims=True)
    )
    return d_values, jnp.sum(upstream * values * inverse, axis=0)


def rotate(values, cosine, sine):
    half = values.shape[-1] // 2
    first, second = values[..., :half], values[..., half:]
    return jnp.concatenate(
        [first * cosine - second * sine, second * cosine + first * sine], axis=-1
    )


def dot(left, right):
    return jnp.dot(left, right, preferred_element_type=F32)


def dot_nt(left, right):
    return lax.dot_general(left, right, (((1,), (1,)), ((), ())), preferred_element_type=F32)


def dot_tn(left, right):
    return lax.dot_general(left, right, (((0,), (0,)), ((), ())), preferred_element_type=F32)


GELU_A = 0.7978845608028654
GELU_B = 0.044715


def gelu(gate):
    return 0.5 * gate * (1.0 + jnp.tanh(GELU_A * (gate + GELU_B * gate * gate * gate)))


def gelu_and_slope(gate):
    square = gate * gate
    bent = jnp.tanh(GELU_A * (gate + GELU_B * gate * square))
    half = 0.5 * (1.0 + bent)
    slope = half + 0.5 * gate * (1.0 - bent * bent) * GELU_A * (1.0 + 3.0 * GELU_B * square)
    return gate * half, slope


def spec(shape, where):
    return pl.BlockSpec(shape, where)


TILE = 768


def call(body, grid, in_specs, out_specs, out_shape, flops, moved, name, limit=44):
    return pl.pallas_call(
        body,
        grid=(grid,),
        in_specs=in_specs,
        out_specs=out_specs,
        out_shape=out_shape,
        compiler_params=pltpu.CompilerParams(
            dimension_semantics=("arbitrary",), vmem_limit_bytes=limit << 20
        ),
        cost_estimate=pl.CostEstimate(flops=flops, bytes_accessed=moved, transcendentals=0),
        name=name,
    )


def held_kernel(*refs):
    pass


def held(value, *deps):
    return pl.pallas_call(
        held_kernel,
        in_specs=[pl.BlockSpec(memory_space=pl.ANY)] * (1 + len(deps)),
        out_specs=pl.BlockSpec(memory_space=pl.ANY),
        out_shape=jax.ShapeDtypeStruct(value.shape, value.dtype),
        input_output_aliases={0: 0},
        compiler_params=pltpu.CompilerParams(has_side_effects=True),
        name="held",
    )(value, *deps)


def gate_up_kernel(x_ref, gate_ref, up_ref, gate_out, up_out, activ_out):
    gate = dot(x_ref[...], gate_ref[...])
    up = dot(x_ref[...], up_ref[...])
    gate_out[...] = gate
    up_out[...] = up
    activ_out[...] = (gelu(gate) * up).astype(BF16)


def gate_up(x, weights):
    rows, depth = x.shape
    units = weights.shape[1] // 2
    tiles = units // TILE
    tile = spec((rows, TILE), lambda j: (0, j))
    return call(
        gate_up_kernel,
        tiles,
        [
            spec((rows, depth), lambda j: (0, 0)),
            spec((depth, TILE), lambda j: (0, j)),
            spec((depth, TILE), lambda j: (0, j + tiles)),
        ],
        (tile, tile, tile),
        tuple(jax.ShapeDtypeStruct((rows, units), kind) for kind in (F32, F32, BF16)),
        4 * rows * depth * units,
        4 * depth * units + 12 * rows * units,
        "gate_up",
    )(x, weights, weights)


def down_kernel(x_ref, w_ref, out_ref):
    out_ref[...] = dot_nt(x_ref[...], w_ref[...]).astype(out_ref.dtype)


def down(x, weights):
    rows, units = x.shape
    width = weights.shape[0]
    return call(
        down_kernel,
        width // TILE,
        [spec((rows, units), lambda j: (0, 0)), spec((TILE, units), lambda j: (j, 0))],
        spec((rows, TILE), lambda j: (0, j)),
        jax.ShapeDtypeStruct((rows, width), BF16),
        2 * rows * width * units,
        2 * width * units,
        "down",
    )(x, weights)


def d_activ_kernel(x_ref, w_ref, gate_ref, up_ref, d_gate_ref, d_up_ref):
    d_activ = dot(x_ref[...], w_ref[...])
    bent, slope = gelu_and_slope(gate_ref[...])
    d_gate_ref[...] = (d_activ * up_ref[...] * slope).astype(BF16)
    d_up_ref[...] = (d_activ * bent).astype(BF16)


def d_gate_up(x, weights, gate_lin, up_lin):
    rows, width = x.shape
    units = weights.shape[1]
    tile = spec((rows, TILE), lambda j: (0, j))
    return call(
        d_activ_kernel,
        units // TILE,
        [
            spec((rows, width), lambda j: (0, 0)),
            spec((width, TILE), lambda j: (0, j)),
            tile,
            tile,
        ],
        (tile, tile),
        tuple(jax.ShapeDtypeStruct((rows, units), BF16) for _ in range(2)),
        2 * rows * width * units,
        2 * width * units + 12 * rows * units,
        "d_gate_up",
    )(x, weights, gate_lin, up_lin)


def d_normed_kernel(a_ref, b_ref, wa_ref, wb_ref, out_ref):
    total = dot_nt(a_ref[...], wa_ref[...]) + dot_nt(b_ref[...], wb_ref[...])
    out_ref[...] = total.astype(out_ref.dtype)


def d_normed_of(d_gate, d_up, weights):
    rows, units = d_gate.shape
    width = weights.shape[0]
    whole = spec((rows, units), lambda j: (0, 0))
    return call(
        d_normed_kernel,
        width // TILE,
        [
            whole,
            whole,
            spec((TILE, units), lambda j: (j, 0)),
            spec((TILE, units), lambda j: (j, 1)),
        ],
        spec((rows, TILE), lambda j: (0, j)),
        jax.ShapeDtypeStruct((rows, width), BF16),
        4 * rows * width * units,
        4 * width * units,
        "d_normed",
    )(d_gate, d_up, weights, weights)


def outer_kernel(a_ref, b_ref, out_ref):
    out_ref[...] = dot_tn(a_ref[...], b_ref[...]).astype(out_ref.dtype)


def outer(left, right, name):
    rows, width = left.shape
    units = right.shape[1]
    return call(
        outer_kernel,
        width // TILE,
        [spec((rows, TILE), lambda j: (0, j)), spec((rows, units), lambda j: (0, 0))],
        spec((TILE, units), lambda j: (j, 0)),
        jax.ShapeDtypeStruct((width, units), BF16),
        2 * rows * width * units,
        2 * width * units,
        name,
    )(left, right)


def outer_pair_kernel(a_ref, b_ref, c_ref, *rest):
    out_ref, mark_ref = rest[-2:]
    mark_ref[...] = jnp.zeros(mark_ref.shape, mark_ref.dtype)
    units = b_ref.shape[1]
    out_ref[:, :units] = dot_tn(a_ref[...], b_ref[...]).astype(out_ref.dtype)
    out_ref[:, units:] = dot_tn(a_ref[...], c_ref[...]).astype(out_ref.dtype)


def outer_pair(left, right, other, begun, name):
    rows, width = left.shape
    units = right.shape[1]
    whole = spec((rows, units), lambda j: (0, 0))
    tiles = width // TILE
    most = tiles - tiles // 2
    start, grid = (0, most) if begun is None else (most, tiles - most)
    more = [] if begun is None else [begun]
    return pl.pallas_call(
        outer_pair_kernel,
        grid=(grid,),
        in_specs=[spec((rows, TILE), lambda j: (0, j + start)), whole, whole]
        + [pl.BlockSpec(memory_space=pl.ANY)] * len(more),
        out_specs=(
            spec((TILE, 2 * units), lambda j: (j + start, 0)),
            spec((8, 128), lambda j: (0, 0)),
        ),
        out_shape=(
            jax.ShapeDtypeStruct((width, 2 * units), BF16),
            jax.ShapeDtypeStruct((8, 128), F32),
        ),
        input_output_aliases={3: 0} if more else {},
        compiler_params=pltpu.CompilerParams(
            dimension_semantics=("arbitrary",), vmem_limit_bytes=44 << 20
        ),
        cost_estimate=pl.CostEstimate(
            flops=4 * rows * grid * TILE * units,
            bytes_accessed=4 * grid * TILE * units,
            transcendentals=0,
        ),
        name=name,
    )(left, right, other, *more)


def outer_two_kernel(a_ref, b_ref, c_ref, d_ref, more_ref, out_ref):
    units = b_ref.shape[1]
    both = units + d_ref.shape[1]
    out_ref[:, :units] = dot_tn(a_ref[...], b_ref[...]).astype(out_ref.dtype)
    out_ref[:, units:both] = dot_tn(c_ref[...], d_ref[...]).astype(out_ref.dtype)
    out_ref[:, both:] = more_ref[...].astype(out_ref.dtype)


def outer_two(left, right, left_b, right_b, extra, name):
    rows, width = left.shape
    units, more = right.shape[1], right_b.shape[1]
    side = spec((rows, TILE), lambda j: (0, j))
    return call(
        outer_two_kernel,
        width // TILE,
        [
            side,
            spec((rows, units), lambda j: (0, 0)),
            side,
            spec((rows, more), lambda j: (0, 0)),
            spec((TILE, extra.shape[1]), lambda j: (j, 0)),
        ],
        spec((TILE, units + more + extra.shape[1]), lambda j: (j, 0)),
        jax.ShapeDtypeStruct((width, units + more + extra.shape[1]), BF16),
        2 * rows * width * (units + more),
        2 * width * (units + more),
        name,
    )(left, right, left_b, right_b, extra)


def stack_heads(ref, rows, first, count):
    return jnp.concatenate(
        [ref[rows, pl.ds((first + h) * HEAD_DIM, HEAD_DIM)] for h in range(count)], axis=0
    )


def attend_kernel(heads, info, q_ref, kv_ref, qseg_ref, kseg_ref, out_ref, inv_ref, p_ref):
    low, high = info[0], info[1]
    rows = heads * BLOCK
    every = pl.ds(0, BLOCK)
    query = stack_heads(q_ref, every, 0, heads)
    qseg = jnp.concatenate([qseg_ref[...]] * heads, axis=0)

    def first(j, acc):
        start = pl.multiple_of(info[2 + j] * BLOCK, BLOCK)
        scores = dot_nt(query, kv_ref[pl.ds(start, BLOCK), pl.ds(0, HEAD_DIM)])
        weight = jnp.exp(CAP * jnp.tanh(scores * (1.0 / CAP)))
        weight = jnp.where(qseg == kseg_ref[pl.ds(j, 1), :], weight, 0.0)
        p_ref[j] = weight
        return acc + weight[:, :128] + weight[:, 128:]

    acc = lax.fori_loop(low, high + 1, first, jnp.zeros((rows, 128), F32))
    inverse = 1.0 / jnp.sum(acc, axis=1, keepdims=True)
    inv_ref[...] = inverse

    def second(j, total):
        start = pl.multiple_of(info[2 + j] * BLOCK, BLOCK)
        low_probs = (p_ref[j] * inverse).astype(BF16)
        return total + dot(low_probs, kv_ref[pl.ds(start, BLOCK), pl.ds(HEAD_DIM, HEAD_DIM)])

    total = lax.fori_loop(low, high + 1, second, jnp.zeros((rows, HEAD_DIM), F32))
    for h in range(heads):
        out_ref[:, pl.ds(h * HEAD_DIM, HEAD_DIM)] = total[h * BLOCK : (h + 1) * BLOCK].astype(BF16)


def vmem():
    return pl.BlockSpec(memory_space=pltpu.VMEM)


def attend(info, queries, kv, qseg, kseg, heads):
    blocks = kseg.shape[0]
    return pl.pallas_call(
        functools.partial(attend_kernel, heads),
        out_shape=(
            jax.ShapeDtypeStruct((BLOCK, heads * HEAD_DIM), BF16),
            jax.ShapeDtypeStruct((heads * BLOCK, 1), F32),
        ),
        in_specs=[pl.BlockSpec(memory_space=pltpu.SMEM)] + [vmem()] * 4,
        out_specs=(vmem(), vmem()),
        scratch_shapes=[pltpu.VMEM((blocks, heads * BLOCK, BLOCK), F32)],
        compiler_params=pltpu.CompilerParams(vmem_limit_bytes=(16 if blocks <= 8 else 48) << 20),
        cost_estimate=pl.CostEstimate(
            flops=3 * heads * BLOCK * blocks * BLOCK * HEAD_DIM,
            bytes_accessed=4 << 20,
            transcendentals=heads * BLOCK * blocks * BLOCK,
        ),
        name="attend",
    )(info, queries, kv, qseg, kseg)


def attend_back_kernel(
    heads, each, info, q_ref, do_ref, kv_ref, inv_ref, qseg_ref, kseg_ref, dq_ref, dkv_ref,
    p_ref, g_ref, dp_ref,
):
    blocks_q = q_ref.shape[0] // BLOCK
    dkv_ref[...] = jnp.zeros(dkv_ref.shape, F32)
    keys = pl.ds(0, HEAD_DIM)
    vals = pl.ds(HEAD_DIM, HEAD_DIM)
    for i in range(blocks_q):
        low, high = info[2 * i], info[2 * i + 1]
        qrows = pl.ds(i * BLOCK, BLOCK)
        qseg = jnp.concatenate([qseg_ref[qrows, :]] * each, axis=0)
        for h in range(0, heads, each):
            query = stack_heads(q_ref, qrows, h, each)
            d_out = stack_heads(do_ref, qrows, h, each)
            inverse = inv_ref[pl.ds((i * heads + h) * BLOCK, each * BLOCK), :]

            def first(j, acc, query=query, d_out=d_out, inverse=inverse, qseg=qseg):
                start = pl.multiple_of(info[2 * blocks_q + j] * BLOCK, BLOCK)
                place = pl.ds(start, BLOCK)
                bent = jnp.tanh(dot_nt(query, kv_ref[place, keys]) * (1.0 / CAP))
                probs = jnp.exp(CAP * bent) * inverse
                probs = jnp.where(qseg == kseg_ref[pl.ds(j, 1), :], probs, 0.0)
                d_probs = dot_nt(d_out, kv_ref[place, vals])
                p_ref[j] = probs.astype(BF16)
                g_ref[j] = probs * (1.0 - bent * bent)
                dp_ref[j] = d_probs
                both = probs * d_probs
                return acc + both[:, :128] + both[:, 128:]

            acc = lax.fori_loop(low, high + 1, first, jnp.zeros((each * BLOCK, 128), F32))
            inner = jnp.sum(acc, axis=1, keepdims=True)

            def second(j, total, query=query, d_out=d_out, inner=inner):
                start = pl.multiple_of(info[2 * blocks_q + j] * BLOCK, BLOCK)
                place = pl.ds(start, BLOCK)
                d_scores = (g_ref[j] * (dp_ref[j] - inner)).astype(BF16)
                dkv_ref[place, keys] += dot_tn(d_scores, query)
                dkv_ref[place, vals] += dot_tn(p_ref[j], d_out)
                return total + dot(d_scores, kv_ref[place, keys])

            total = lax.fori_loop(
                low, high + 1, second, jnp.zeros((each * BLOCK, HEAD_DIM), F32)
            )
            for n in range(each):
                dq_ref[qrows, pl.ds((h + n) * HEAD_DIM, HEAD_DIM)] = total[
                    n * BLOCK : (n + 1) * BLOCK
                ]


def attend_back(info, queries, d_out, kv, inverse, qseg, kseg, heads):
    blocks = kseg.shape[0]
    each = heads if blocks <= 8 else 1
    tile = (blocks, each * BLOCK, BLOCK)
    return pl.pallas_call(
        functools.partial(attend_back_kernel, heads, each),
        out_shape=(
            jax.ShapeDtypeStruct(queries.shape, F32),
            jax.ShapeDtypeStruct(kv.shape, F32),
        ),
        in_specs=[pl.BlockSpec(memory_space=pltpu.SMEM)] + [vmem()] * 6,
        out_specs=(vmem(), vmem()),
        scratch_shapes=[pltpu.VMEM(tile, BF16), pltpu.VMEM(tile, F32), pltpu.VMEM(tile, F32)],
        compiler_params=pltpu.CompilerParams(vmem_limit_bytes=(26 if blocks <= 8 else 56) << 20),
        cost_estimate=pl.CostEstimate(
            flops=11 * heads * BLOCK * blocks * BLOCK * HEAD_DIM,
            bytes_accessed=10 << 20,
            transcendentals=2 * heads * BLOCK * blocks * BLOCK,
        ),
        name="attend_back",
    )(info, queries, d_out, kv, inverse, qseg, kseg)


def per_device(
    sizes,
    tokens,
    q_weight,
    key_weight,
    value_weight,
    out_weight,
    gate_weight,
    up_weight,
    down_weight,
    gain_attn_in,
    gain_attn_out,
    gain_mlp_in,
    gain_mlp_out,
    segment_ids,
    block_order,
    cotangent,
):
    tp = sizes["tp"]
    wide = Ring(sizes, ("fsdp", "ctx"))
    near = Ring(sizes, ("ctx",))
    group = 2 * wide.count
    here = lax.axis_index("tp")
    tok = tokens[0]
    count, width = tok.shape
    halves = count // BLOCK
    share = BLOCK // tp
    heads = q_weight.shape[1] // HEAD_DIM
    qcols = q_weight.shape[1]

    split = ("fsdp", "ctx")
    gains_own = jnp.stack([gain_attn_in, gain_attn_out, gain_mlp_in, gain_mlp_out])
    gains_own = jnp.pad(gains_own, ((0, 124), (0, 0))).T
    attn_own = jnp.concatenate(
        [q_weight, key_weight, value_weight, out_weight.T, gains_own], axis=1
    )
    attn_w = lax.all_gather(attn_own, split, axis=0, tiled=True)
    gu_own = jnp.concatenate([gate_weight, after(up_weight, attn_own)], axis=1)
    gu_w = lax.all_gather(after(gu_own, attn_w), split, axis=0, tiled=True)
    down_own = after(down_weight, gu_own).T
    lin_cols = qcols + 2 * HEAD_DIM
    out_cols = lin_cols + out_weight.shape[0]
    qkv_w, out_w = attn_w[:, :lin_cols], attn_w[:, lin_cols:out_cols]
    gains = attn_w[:, out_cols : out_cols + 4].T.astype(F32)
    gain_one, gain_two, gain_three, gain_four = (gains[i] for i in range(4))

    order = block_order[0]
    blocks = order.shape[0]
    stored = jnp.argsort(order).astype(jnp.int32)
    segs = segment_ids[0].reshape(blocks, BLOCK)
    first_block = lax.axis_index("ctx") * halves
    high = lax.dynamic_slice_in_dim(order, first_block, halves)
    qsegs = segs[high]
    low = jnp.sum((segs[None, :, -1] < qsegs[:, :1]).astype(jnp.int32), axis=1)
    bounds = jnp.stack([low, high], axis=1).astype(jnp.int32)
    infos = [jnp.concatenate([bounds[i], stored]) for i in range(halves)]
    info_all = jnp.concatenate([bounds.reshape(-1), stored])
    qseg = qsegs.reshape(count, 1)

    spot = (high[:, None] * BLOCK + jnp.arange(BLOCK, dtype=jnp.int32)[None]).reshape(-1)
    half_dim = HEAD_DIM // 2
    freqs = THETA ** (-jnp.arange(half_dim, dtype=F32) * 2.0 / HEAD_DIM)
    angles = spot.astype(F32)[:, None] * freqs[None, :]
    cosine, sine = jnp.cos(angles), jnp.sin(angles)
    scale = HEAD_DIM**-0.5

    inputs = tok.astype(F32)
    inv_one = inverse_of(inputs)
    normed_attn = (inputs * inv_one * gain_one).astype(BF16)
    lin = dot(normed_attn, qkv_w)
    q_lin = lin[:, :qcols].reshape(count, heads, HEAD_DIM)
    queries = (rotate(q_lin, cosine[:, None], sine[:, None]) * scale).astype(BF16)
    queries = queries.reshape(count, qcols)
    keys = rotate(lin[:, qcols : qcols + HEAD_DIM], cosine, sine).astype(BF16)
    values = lin[:, qcols + HEAD_DIM :].astype(BF16)
    kv_own = jnp.concatenate([keys, values], axis=1)
    kv_move = begun(gather_steps(near, kv_own))
    for _ in range(near.count - 1):
        kv = step(kv_move, queries, qseg, *infos)
    down_move = gather_steps(wide, down_own, attn_w)
    passing = next(down_move)
    down_left = wide.count - 1

    def pass_down(*waits):
        nonlocal passing, down_left
        if down_left:
            passing, down_left = step(down_move, *waits), down_left - 1

    pass_down(kv)

    def rows_of(array, i):
        return lax.slice_in_dim(array, i * BLOCK, (i + 1) * BLOCK)

    def share_of(array, i):
        return lax.dynamic_slice_in_dim(array, i * BLOCK + here * share, share).astype(F32)

    def joined(pieces):
        return jnp.concatenate(pieces, axis=0)

    hops = tp - 1
    both = range(halves)

    def all_steps(parts):
        for _ in range(hops):
            last = [step(part) for part in parts]
        return last

    attended, inverse_sum, sums = [], [], []
    for i in both:
        out, inv = attend(infos[i], rows_of(queries, i), kv, rows_of(qseg, i), segs, heads)
        attended.append(out)
        inverse_sum.append(inv)
        sums.append(tp_scatter(dot_nt(out, out_w).astype(BF16), tp))
        next(sums[i])
    for n in range(hops):
        branch_attn = [step(part) for part in sums]
        if n == 1:
            pass_down(*branch_attn)
    inv_two = [inverse_of(branch) for branch in branch_attn]
    resid = [share_of(tok, i) + branch_attn[i] * inv_two[i] * gain_two for i in both]
    inv_three = [inverse_of(value) for value in resid]
    moves = [tp_gather((resid[i] * inv_three[i] * gain_three).astype(BF16), tp) for i in both]
    for move in moves:
        next(move)
    for n in range(hops - 1):
        sent = [step(move) for move in moves]
    first = step(moves[0])

    gate_lin, up_lin, activ = [None] * halves, [None] * halves, [None] * halves
    gate_lin[0], up_lin[0], activ[0] = gate_up(after(first, sent[-1]), gu_w)
    normed_mlp = [first] + [step(move, activ[0]) for move in moves[1:]]
    while down_left:
        pass_down(activ[0])
    down_w = passing
    sums = [tp_scatter(down(activ[0], down_w), tp)]
    sent = next(sums[0])
    gate_lin[1], up_lin[1], activ[1] = gate_up(after(normed_mlp[1], sent), gu_w)
    sent = step(sums[0], activ[1])
    part = down(after(activ[1], sent), down_w)
    sums.append(tp_scatter(part, tp))
    next(sums[1])
    sent = step(sums[0], part)

    layer_own, grad_four, moves = [], [], []

    def middle(i, branch):
        inv = inverse_of(branch)
        layer_own.append((resid[i] + branch * inv * gain_four).astype(BF16))
        d_branch, d_gain = norm_back(branch, inv, gain_four, share_of(cotangent[0], i))
        grad_four.append(d_gain)
        moves.append(tp_gather(d_branch.astype(BF16), tp))
        return next(moves[i])

    step(sums[1])
    middle(0, step(sums[0]))
    step(sums[1])
    step(moves[0])
    middle(1, step(sums[1]))
    step(moves[0])
    step(moves[1])
    first = step(moves[0])
    sent = step(moves[1])
    d_gate, d_up = [None] * halves, [None] * halves
    d_mlp_low = [first, step(moves[1])]
    grad_down = outer(joined(d_mlp_low), joined(activ), "grad_down")
    d_gate[0], d_up[0] = d_gate_up(after(first, grad_down), down_w, gate_lin[0], up_lin[0])
    part = d_normed_of(after(d_gate[0], grad_down), d_up[0], gu_w)
    sums = [tp_scatter(part, tp)]
    sent = next(sums[0])
    d_gate[1], d_up[1] = d_gate_up(after(d_mlp_low[1], sent), down_w, gate_lin[1], up_lin[1])
    sent = step(sums[0], d_gate[1])
    part = d_normed_of(after(d_gate[1], sent), d_up[1], gu_w)
    sums.append(tp_scatter(part, tp))
    sent = next(sums[1]), step(sums[0], part)
    d_resid, grad_three, grad_two, moves = [], [], [], []

    def middle_back(i, part):
        d_in, d_gain = norm_back(resid[i], inv_three[i], gain_three, part)
        grad_three.append(d_gain)
        d_resid.append(share_of(cotangent[0], i) + d_in)
        d_branch, d_gain = norm_back(branch_attn[i], inv_two[i], gain_two, d_resid[i])
        grad_two.append(d_gain)
        moves.append(tp_gather(d_branch.astype(BF16), tp))
        return next(moves[i])

    normed_all = joined(normed_mlp)
    d_pair = joined(d_gate), joined(d_up)
    grad_gu, mark = outer_pair(after(normed_all, *sent), *d_pair, None, "grad_gate_up")
    sent = middle_back(0, step(sums[0], mark)), step(sums[1], mark)
    grad_gu, mark = outer_pair(after(normed_all, *sent), *d_pair, grad_gu, "grad_gate_up_more")
    sent = step(sums[1], mark), step(moves[0], mark)
    grad_down = lax.psum_scatter(grad_down, split, scatter_dimension=0, tiled=True)
    middle_back(1, step(sums[1]))
    grad_gu = held(grad_gu, grad_down, *sent)
    grad_gu = lax.psum_scatter(grad_gu, split, scatter_dimension=0, tiled=True)
    grad_down = grad_down.astype(F32)
    step(moves[0])
    step(moves[1])
    first = step(moves[0])
    d_attn_low = [first, finish(moves[1], hops - 1)]

    d_attn_all = joined(d_attn_low)
    d_attended = dot(d_attn_all, out_w).astype(BF16)
    d_queries, d_kv = attend_back(
        info_all, queries, d_attended, kv, joined(inverse_sum), qseg, segs, heads
    )
    kv_move = scatter_steps(near, d_kv, BF16)
    d_queries = after(d_queries, next(kv_move))
    d_q_lin = rotate(
        d_queries.reshape(count, heads, HEAD_DIM) * scale, cosine[:, None], -sine[:, None]
    ).astype(BF16)
    d_q_lin = d_q_lin.reshape(count, qcols)
    layer_move = begun(tp_gather(after(jnp.stack(layer_own), d_attn_all), tp))
    passing = step(layer_move, d_kv)
    from_q = dot_nt(after(d_q_lin, passing), qkv_w[:, :qcols])
    passing = step(layer_move, from_q)
    for _ in range(near.count - 1):
        d_kv = step(kv_move, passing)
    d_key_lin = rotate(d_kv[:, :HEAD_DIM], cosine, -sine).astype(BF16)
    d_kv_lin = jnp.concatenate([d_key_lin, d_kv[:, HEAD_DIM:].astype(BF16)], axis=1)
    d_normed_attn = from_q + dot_nt(d_kv_lin, qkv_w[:, qcols:])
    d_normed_low = d_normed_attn.astype(BF16)
    sums = [tp_scatter(rows_of(d_normed_low, i), tp) for i in both]
    sent = [next(part) for part in sums]
    grad_one = jnp.sum(after(d_normed_attn, *sent) * inputs * inv_one, axis=0)
    grad_gains = [grad_one, sum(grad_two), sum(grad_three), sum(grad_four)]
    grad_gains = jnp.stack(grad_gains + [jnp.zeros_like(grad_one)] * 4)
    left, bit = hops, 1
    while bit < tp:
        got = lax.ppermute(grad_gains, "tp", [(i, i ^ bit) for i in range(tp)])
        if left > 1:
            sent, left = [step(part) for part in sums], left - 1
        grad_gains = grad_gains + after(got, *sent)
        bit *= 2
    grad_gains = jnp.pad(grad_gains, ((0, 120), (0, 0))).T
    d_lin = jnp.concatenate([d_q_lin, d_kv_lin], axis=1)
    grad_attn = outer_two(
        normed_attn, d_lin, d_attn_all, joined(attended), grad_gains, "grad_attn"
    )
    grad_attn = held(grad_attn, grad_gu, *sent)
    for _ in range(left):
        sent = [step(part) for part in sums]
    grad_attn = lax.psum_scatter(grad_attn, split, scatter_dimension=0, tiled=True).astype(F32)
    grad_gu = grad_gu.astype(F32)
    moves = []
    for i in both:
        own = share_of(tok, i)
        d_in, unused = norm_back(own, inverse_of(own), gain_one, sent[i])
        moves.append(begun(tp_gather((d_resid[i] + d_in).astype(BF16), tp, F32)))
    for n in range(hops):
        grad_tokens = [step(move) for move in moves]
        if n == hops - 2:
            layer_out = step(layer_move, *grad_tokens)
    grad_gains = grad_attn[:, out_cols : out_cols + 4].T
    grad_qkv, grad_out = grad_attn[:, :lin_cols], grad_attn[:, lin_cols:out_cols]

    return (
        layer_out.reshape(1, count, width),
        joined(grad_tokens)[None],
        grad_qkv[:, :qcols],
        grad_qkv[:, qcols : qcols + HEAD_DIM],
        grad_qkv[:, qcols + HEAD_DIM :],
        grad_out.T,
        grad_gu[:, : gate_weight.shape[1]],
        grad_gu[:, gate_weight.shape[1] :],
        grad_down.T,
        grad_gains[0],
        grad_gains[1],
        grad_gains[2],
        grad_gains[3],
    )


def solution(mesh):
    sizes = dict(mesh.shape)
    split = ("fsdp", "ctx")
    rows, cols = P(split, "tp"), P("tp", split)
    acts, ids = P("fsdp", "ctx", None), P("fsdp", None)
    return jax.shard_map(
        functools.partial(per_device, sizes),
        mesh=mesh,
        in_specs=(acts, rows, rows, rows, cols, rows, rows, cols)
        + (P(split),) * 4
        + (ids, ids, acts),
        out_specs=(acts, acts, rows, rows, rows, cols, rows, rows, cols) + (P(split),) * 4,
        check_vma=False,
    )
```

```python
import functools

import jax
import jax.numpy as jnp
import numpy as np
from jax import lax
from jax.experimental import pallas as pl
from jax.experimental.pallas import tpu as pltpu
from jax.sharding import PartitionSpec as P

HEAD_DIM = 256
BLOCK = 256
EPS = 1e-06
CAP = 50.0
THETA = 10000.0
F32 = jnp.float32
BF16 = jnp.bfloat16


class Ring:
    def __init__(self, sizes, axes):
        self.axes = axes
        outer = sizes[axes[0]] if len(axes) == 2 else 1
        inner = sizes[axes[-1]] // 2
        order = []
        for row in range(outer):
            cols = range(inner) if row % 2 == 0 else reversed(range(inner))
            order += [row * inner + col for col in cols]
        self.order = np.array(order, np.int32)
        self.count = len(order)
        self.place = np.argsort(self.order).astype(np.int32)
        self.sibling = [(i, i ^ 1) for i in range(2 * self.count)]

    def pairs(self, sign):
        out = []
        for pos in range(self.count):
            for core in range(2):
                step = sign if core == 0 else -sign
                there = self.order[(pos + step) % self.count]
                out.append((int(self.order[pos]) * 2 + core, int(there) * 2 + core))
        return out

    def locate(self):
        me = lax.axis_index(self.axes)
        core = me % 2
        pos = jnp.asarray(self.place)[me // 2]
        return pos, core

    def owner(self, pos, core, label):
        step = jnp.where(core == 0, label, -label)
        return jnp.asarray(self.order)[(pos + step) % self.count] * 2 + core

    def swap(self, value):
        return lax.ppermute(value, self.axes, self.sibling)


def after(value, *deps):
    return lax.optimization_barrier((value,) + deps)[0]


def put(buffer, piece, index):
    starts = (index * piece.shape[0],) + (0,) * (buffer.ndim - 1)
    return lax.dynamic_update_slice(buffer, piece, starts)


def blank_kernel(ref):
    pass


def blank(shape, kind):
    return pl.pallas_call(
        blank_kernel,
        out_specs=pl.BlockSpec(memory_space=pl.ANY),
        out_shape=jax.ShapeDtypeStruct(shape, kind),
        compiler_params=pltpu.CompilerParams(has_side_effects=True),
        name="blank",
    )()


def put_two_kernel(spots, whole_ref, one_ref, two_ref, out_ref, sems):
    rows = one_ref.shape[0]
    copies = []
    for n, ref in enumerate((one_ref, two_ref)):
        start = pl.multiple_of(spots[n] * rows, 16)
        copies.append(pltpu.make_async_copy(ref, out_ref.at[pl.ds(start, rows)], sems.at[n]))
    for copy in copies:
        copy.start()
    for copy in copies:
        copy.wait()


def put_two(whole, one, spot, two, other_spot):
    if one.shape[0] % 16:
        return put(put(whole, one, spot), two, other_spot)
    anywhere = pl.BlockSpec(memory_space=pl.ANY)
    return pl.pallas_call(
        put_two_kernel,
        in_specs=[pl.BlockSpec(memory_space=pltpu.SMEM), anywhere, vmem(), vmem()],
        out_specs=anywhere,
        out_shape=jax.ShapeDtypeStruct(whole.shape, whole.dtype),
        scratch_shapes=[pltpu.SemaphoreType.DMA((2,))],
        input_output_aliases={1: 0},
        cost_estimate=pl.CostEstimate(flops=0, bytes_accessed=8 * one.size, transcendentals=0),
        name="put_two",
    )(jnp.stack([spot, other_spot]).astype(jnp.int32), whole, one, two)


def gather_steps(ring, shard, first=None):
    pos, core = ring.locate()
    whole = blank((2 * ring.count * shard.shape[0],) + shard.shape[1:], shard.dtype)
    piece = shard
    for label in range(ring.count):
        if label:
            if label == 1 and first is not None:
                piece = after(piece, first)
            waits = yield piece
            piece = lax.ppermute(piece, ring.axes, ring.pairs(-1))
            if waits:
                piece = after(piece, *waits)
        other = ring.swap(piece)
        spots = ring.owner(pos, core, label), ring.owner(pos, 1 - core, label)
        if first is None:
            whole = put_two(whole, piece, spots[0], other, spots[1])
        else:
            whole = put(put(whole, piece, spots[0]), other, spots[1])
    yield whole


def scatter_steps(ring, value, wire):
    pos, core = ring.locate()
    rows = value.shape[0] // (2 * ring.count)

    def block(kind, label):
        start = ring.owner(pos, kind, label) * rows
        return lax.dynamic_slice_in_dim(value, start, rows).astype(wire)

    labels = range(ring.count)
    other = [ring.swap(block(1 - core, label)) for label in labels]

    def both(label):
        return block(core, label).astype(F32) + other[label].astype(F32)

    total = both(ring.count - 1)
    for label in range(ring.count - 2, -1, -1):
        total = total.astype(wire)
        waits = yield total
        got = lax.ppermute(total, ring.axes, ring.pairs(1))
        if waits:
            got = after(got, *waits)
        total = both(label) + got.astype(F32)
    yield total


def scatter(ring, value, wire):
    return finish(begun(scatter_steps(ring, value, wire)), ring.count - 1)


def tp_pairs(count):
    return [(i, (i + 1) % count) for i in range(count)]


def tp_scatter(part, count):
    here = lax.axis_index("tp")
    rows = part.shape[0] // count

    def chunk(back):
        return lax.dynamic_slice_in_dim(part, ((here - back) % count) * rows, rows)

    total = chunk(1).astype(BF16)
    for step in range(1, count):
        waits = yield total
        got = lax.ppermute(total, "tp", tp_pairs(count))
        if waits:
            got = after(got, *waits)
        total = chunk(step + 1).astype(F32) + got.astype(F32)
        if step + 1 < count:
            total = total.astype(BF16)
    yield total


def tp_gather(own, count, kind=BF16):
    here = lax.axis_index("tp")
    axis = own.ndim - 2
    rows = own.shape[axis]
    shape = own.shape[:axis] + (count * rows,) + own.shape[axis + 1 :]

    def place(whole, piece, index):
        return lax.dynamic_update_slice_in_dim(whole, piece.astype(kind), index * rows, axis)

    whole = place(jnp.zeros(shape, kind), own, here)
    piece = own
    for step in range(1, count):
        waits = yield piece
        piece = lax.ppermute(piece, "tp", tp_pairs(count))
        if waits:
            piece = after(piece, *waits)
        whole = place(whole, piece, (here - step) % count)
    yield whole


def step(steps, *waits):
    return steps.send(waits)


def begun(steps):
    next(steps)
    return steps


def finish(steps, count):
    for _ in range(count):
        last = step(steps)
    return last


def inverse_of(values):
    return lax.rsqrt(jnp.mean(values * values, axis=-1, keepdims=True) + EPS)


def norm_back(values, inverse, gain, upstream):
    scaled = upstream * gain
    d_values = inverse * scaled - values * (
        inverse * inverse * inverse * jnp.mean(scaled * values, axis=-1, keepdims=True)
    )
    return d_values, jnp.sum(upstream * values * inverse, axis=0)


def rotate(values, cosine, sine):
    half = values.shape[-1] // 2
    first, second = values[..., :half], values[..., half:]
    return jnp.concatenate(
        [first * cosine - second * sine, second * cosine + first * sine], axis=-1
    )


def dot(left, right):
    return jnp.dot(left, right, preferred_element_type=F32)


def dot_nt(left, right):
    return lax.dot_general(left, right, (((1,), (1,)), ((), ())), preferred_element_type=F32)


def dot_tn(left, right):
    return lax.dot_general(left, right, (((0,), (0,)), ((), ())), preferred_element_type=F32)


GELU_A = 0.7978845608028654
GELU_B = 0.044715


def gelu(gate):
    return 0.5 * gate * (1.0 + jnp.tanh(GELU_A * (gate + GELU_B * gate * gate * gate)))


def gelu_and_slope(gate):
    square = gate * gate
    bent = jnp.tanh(GELU_A * (gate + GELU_B * gate * square))
    half = 0.5 * (1.0 + bent)
    slope = half + 0.5 * gate * (1.0 - bent * bent) * GELU_A * (1.0 + 3.0 * GELU_B * square)
    return gate * half, slope


def spec(shape, where):
    return pl.BlockSpec(shape, where)


TILE = 768


def call(body, grid, in_specs, out_specs, out_shape, flops, moved, name, limit=44):
    return pl.pallas_call(
        body,
        grid=(grid,),
        in_specs=in_specs,
        out_specs=out_specs,
        out_shape=out_shape,
        compiler_params=pltpu.CompilerParams(
            dimension_semantics=("arbitrary",), vmem_limit_bytes=limit << 20
        ),
        cost_estimate=pl.CostEstimate(flops=flops, bytes_accessed=moved, transcendentals=0),
        name=name,
    )


def held_kernel(*refs):
    pass


def held(value, *deps):
    return pl.pallas_call(
        held_kernel,
        in_specs=[pl.BlockSpec(memory_space=pl.ANY)] * (1 + len(deps)),
        out_specs=pl.BlockSpec(memory_space=pl.ANY),
        out_shape=jax.ShapeDtypeStruct(value.shape, value.dtype),
        input_output_aliases={0: 0},
        compiler_params=pltpu.CompilerParams(has_side_effects=True),
        name="held",
    )(value, *deps)


def gate_up_kernel(x_ref, gate_ref, up_ref, gate_out, up_out, activ_out):
    gate = dot(x_ref[...], gate_ref[...])
    up = dot(x_ref[...], up_ref[...])
    gate_out[...] = gate
    up_out[...] = up
    activ_out[...] = (gelu(gate) * up).astype(BF16)


def gate_up(x, weights):
    rows, depth = x.shape
    units = weights.shape[1] // 2
    tiles = units // TILE
    tile = spec((rows, TILE), lambda j: (0, j))
    return call(
        gate_up_kernel,
        tiles,
        [
            spec((rows, depth), lambda j: (0, 0)),
            spec((depth, TILE), lambda j: (0, j)),
            spec((depth, TILE), lambda j: (0, j + tiles)),
        ],
        (tile, tile, tile),
        tuple(jax.ShapeDtypeStruct((rows, units), kind) for kind in (F32, F32, BF16)),
        4 * rows * depth * units,
        4 * depth * units + 12 * rows * units,
        "gate_up",
    )(x, weights, weights)


def down_kernel(x_ref, w_ref, out_ref):
    out_ref[...] = dot_nt(x_ref[...], w_ref[...]).astype(out_ref.dtype)


def down(x, weights):
    rows, units = x.shape
    width = weights.shape[0]
    return call(
        down_kernel,
        width // TILE,
        [spec((rows, units), lambda j: (0, 0)), spec((TILE, units), lambda j: (j, 0))],
        spec((rows, TILE), lambda j: (0, j)),
        jax.ShapeDtypeStruct((rows, width), BF16),
        2 * rows * width * units,
        2 * width * units,
        "down",
    )(x, weights)


def d_activ_kernel(x_ref, w_ref, gate_ref, up_ref, d_gate_ref, d_up_ref):
    d_activ = dot(x_ref[...], w_ref[...])
    bent, slope = gelu_and_slope(gate_ref[...])
    d_gate_ref[...] = (d_activ * up_ref[...] * slope).astype(BF16)
    d_up_ref[...] = (d_activ * bent).astype(BF16)


def d_gate_up(x, weights, gate_lin, up_lin):
    rows, width = x.shape
    units = weights.shape[1]
    tile = spec((rows, TILE), lambda j: (0, j))
    return call(
        d_activ_kernel,
        units // TILE,
        [
            spec((rows, width), lambda j: (0, 0)),
            spec((width, TILE), lambda j: (0, j)),
            tile,
            tile,
        ],
        (tile, tile),
        tuple(jax.ShapeDtypeStruct((rows, units), BF16) for _ in range(2)),
        2 * rows * width * units,
        2 * width * units + 12 * rows * units,
        "d_gate_up",
    )(x, weights, gate_lin, up_lin)


def d_normed_kernel(a_ref, b_ref, wa_ref, wb_ref, out_ref):
    total = dot_nt(a_ref[...], wa_ref[...]) + dot_nt(b_ref[...], wb_ref[...])
    out_ref[...] = total.astype(out_ref.dtype)


def d_normed_of(d_gate, d_up, weights):
    rows, units = d_gate.shape
    width = weights.shape[0]
    whole = spec((rows, units), lambda j: (0, 0))
    return call(
        d_normed_kernel,
        width // TILE,
        [
            whole,
            whole,
            spec((TILE, units), lambda j: (j, 0)),
            spec((TILE, units), lambda j: (j, 1)),
        ],
        spec((rows, TILE), lambda j: (0, j)),
        jax.ShapeDtypeStruct((rows, width), BF16),
        4 * rows * width * units,
        4 * width * units,
        "d_normed",
    )(d_gate, d_up, weights, weights)


def outer_kernel(a_ref, b_ref, out_ref):
    out_ref[...] = dot_tn(a_ref[...], b_ref[...]).astype(out_ref.dtype)


def outer(left, right, name):
    rows, width = left.shape
    units = right.shape[1]
    return call(
        outer_kernel,
        width // TILE,
        [spec((rows, TILE), lambda j: (0, j)), spec((rows, units), lambda j: (0, 0))],
        spec((TILE, units), lambda j: (j, 0)),
        jax.ShapeDtypeStruct((width, units), BF16),
        2 * rows * width * units,
        2 * width * units,
        name,
    )(left, right)


def outer_pair_kernel(a_ref, b_ref, c_ref, *rest):
    out_ref, mark_ref = rest[-2:]
    mark_ref[...] = jnp.zeros(mark_ref.shape, mark_ref.dtype)
    units = b_ref.shape[1]
    out_ref[:, :units] = dot_tn(a_ref[...], b_ref[...]).astype(out_ref.dtype)
    out_ref[:, units:] = dot_tn(a_ref[...], c_ref[...]).astype(out_ref.dtype)


def outer_pair(left, right, other, begun, name):
    rows, width = left.shape
    units = right.shape[1]
    whole = spec((rows, units), lambda j: (0, 0))
    tiles = width // TILE
    most = tiles - tiles // 2
    start, grid = (0, most) if begun is None else (most, tiles - most)
    more = [] if begun is None else [begun]
    return pl.pallas_call(
        outer_pair_kernel,
        grid=(grid,),
        in_specs=[spec((rows, TILE), lambda j: (0, j + start)), whole, whole]
        + [pl.BlockSpec(memory_space=pl.ANY)] * len(more),
        out_specs=(
            spec((TILE, 2 * units), lambda j: (j + start, 0)),
            spec((8, 128), lambda j: (0, 0)),
        ),
        out_shape=(
            jax.ShapeDtypeStruct((width, 2 * units), BF16),
            jax.ShapeDtypeStruct((8, 128), F32),
        ),
        input_output_aliases={3: 0} if more else {},
        compiler_params=pltpu.CompilerParams(
            dimension_semantics=("arbitrary",), vmem_limit_bytes=44 << 20
        ),
        cost_estimate=pl.CostEstimate(
            flops=4 * rows * grid * TILE * units,
            bytes_accessed=4 * grid * TILE * units,
            transcendentals=0,
        ),
        name=name,
    )(left, right, other, *more)


def outer_two_kernel(a_ref, b_ref, c_ref, d_ref, more_ref, out_ref):
    units = b_ref.shape[1]
    both = units + d_ref.shape[1]
    out_ref[:, :units] = dot_tn(a_ref[...], b_ref[...]).astype(out_ref.dtype)
    out_ref[:, units:both] = dot_tn(c_ref[...], d_ref[...]).astype(out_ref.dtype)
    out_ref[:, both:] = more_ref[...].astype(out_ref.dtype)


def outer_two(left, right, left_b, right_b, extra, name):
    rows, width = left.shape
    units, more = right.shape[1], right_b.shape[1]
    side = spec((rows, TILE), lambda j: (0, j))
    return call(
        outer_two_kernel,
        width // TILE,
        [
            side,
            spec((rows, units), lambda j: (0, 0)),
            side,
            spec((rows, more), lambda j: (0, 0)),
            spec((TILE, extra.shape[1]), lambda j: (j, 0)),
        ],
        spec((TILE, units + more + extra.shape[1]), lambda j: (j, 0)),
        jax.ShapeDtypeStruct((width, units + more + extra.shape[1]), BF16),
        2 * rows * width * (units + more),
        2 * width * (units + more),
        name,
    )(left, right, left_b, right_b, extra)


def stack_heads(ref, rows, first, count):
    return jnp.concatenate(
        [ref[rows, pl.ds((first + h) * HEAD_DIM, HEAD_DIM)] for h in range(count)], axis=0
    )


def attend_kernel(heads, info, q_ref, kv_ref, qseg_ref, kseg_ref, out_ref, inv_ref, p_ref):
    low, high = info[0], info[1]
    rows = heads * BLOCK
    every = pl.ds(0, BLOCK)
    query = stack_heads(q_ref, every, 0, heads)
    qseg = jnp.concatenate([qseg_ref[...]] * heads, axis=0)

    def first(j, acc):
        start = pl.multiple_of(info[2 + j] * BLOCK, BLOCK)
        scores = dot_nt(query, kv_ref[pl.ds(start, BLOCK), pl.ds(0, HEAD_DIM)])
        weight = jnp.exp(CAP * jnp.tanh(scores * (1.0 / CAP)))
        weight = jnp.where(qseg == kseg_ref[pl.ds(j, 1), :], weight, 0.0)
        p_ref[j] = weight
        return acc + weight[:, :128] + weight[:, 128:]

    acc = lax.fori_loop(low, high + 1, first, jnp.zeros((rows, 128), F32))
    inverse = 1.0 / jnp.sum(acc, axis=1, keepdims=True)
    inv_ref[...] = inverse

    def second(j, total):
        start = pl.multiple_of(info[2 + j] * BLOCK, BLOCK)
        low_probs = (p_ref[j] * inverse).astype(BF16)
        return total + dot(low_probs, kv_ref[pl.ds(start, BLOCK), pl.ds(HEAD_DIM, HEAD_DIM)])

    total = lax.fori_loop(low, high + 1, second, jnp.zeros((rows, HEAD_DIM), F32))
    for h in range(heads):
        out_ref[:, pl.ds(h * HEAD_DIM, HEAD_DIM)] = total[h * BLOCK : (h + 1) * BLOCK].astype(BF16)


def vmem():
    return pl.BlockSpec(memory_space=pltpu.VMEM)


def attend(info, queries, kv, qseg, kseg, heads):
    blocks = kseg.shape[0]
    return pl.pallas_call(
        functools.partial(attend_kernel, heads),
        out_shape=(
            jax.ShapeDtypeStruct((BLOCK, heads * HEAD_DIM), BF16),
            jax.ShapeDtypeStruct((heads * BLOCK, 1), F32),
        ),
        in_specs=[pl.BlockSpec(memory_space=pltpu.SMEM)] + [vmem()] * 4,
        out_specs=(vmem(), vmem()),
        scratch_shapes=[pltpu.VMEM((blocks, heads * BLOCK, BLOCK), F32)],
        compiler_params=pltpu.CompilerParams(vmem_limit_bytes=(16 if blocks <= 8 else 48) << 20),
        cost_estimate=pl.CostEstimate(
            flops=3 * heads * BLOCK * blocks * BLOCK * HEAD_DIM,
            bytes_accessed=4 << 20,
            transcendentals=heads * BLOCK * blocks * BLOCK,
        ),
        name="attend",
    )(info, queries, kv, qseg, kseg)


def attend_back_kernel(
    heads, each, info, q_ref, do_ref, kv_ref, inv_ref, qseg_ref, kseg_ref, dq_ref, dkv_ref,
    p_ref, g_ref, dp_ref,
):
    blocks_q = q_ref.shape[0] // BLOCK
    dkv_ref[...] = jnp.zeros(dkv_ref.shape, F32)
    keys = pl.ds(0, HEAD_DIM)
    vals = pl.ds(HEAD_DIM, HEAD_DIM)
    for i in range(blocks_q):
        low, high = info[2 * i], info[2 * i + 1]
        qrows = pl.ds(i * BLOCK, BLOCK)
        qseg = jnp.concatenate([qseg_ref[qrows, :]] * each, axis=0)
        for h in range(0, heads, each):
            query = stack_heads(q_ref, qrows, h, each)
            d_out = stack_heads(do_ref, qrows, h, each)
            inverse = inv_ref[pl.ds((i * heads + h) * BLOCK, each * BLOCK), :]

            def first(j, acc, query=query, d_out=d_out, inverse=inverse, qseg=qseg):
                start = pl.multiple_of(info[2 * blocks_q + j] * BLOCK, BLOCK)
                place = pl.ds(start, BLOCK)
                bent = jnp.tanh(dot_nt(query, kv_ref[place, keys]) * (1.0 / CAP))
                probs = jnp.exp(CAP * bent) * inverse
                probs = jnp.where(qseg == kseg_ref[pl.ds(j, 1), :], probs, 0.0)
                d_probs = dot_nt(d_out, kv_ref[place, vals])
                p_ref[j] = probs.astype(BF16)
                g_ref[j] = probs * (1.0 - bent * bent)
                dp_ref[j] = d_probs
                both = probs * d_probs
                return acc + both[:, :128] + both[:, 128:]

            acc = lax.fori_loop(low, high + 1, first, jnp.zeros((each * BLOCK, 128), F32))
            inner = jnp.sum(acc, axis=1, keepdims=True)

            def second(j, total, query=query, d_out=d_out, inner=inner):
                start = pl.multiple_of(info[2 * blocks_q + j] * BLOCK, BLOCK)
                place = pl.ds(start, BLOCK)
                d_scores = (g_ref[j] * (dp_ref[j] - inner)).astype(BF16)
                dkv_ref[place, keys] += dot_tn(d_scores, query)
                dkv_ref[place, vals] += dot_tn(p_ref[j], d_out)
                return total + dot(d_scores, kv_ref[place, keys])

            total = lax.fori_loop(
                low, high + 1, second, jnp.zeros((each * BLOCK, HEAD_DIM), F32)
            )
            for n in range(each):
                dq_ref[qrows, pl.ds((h + n) * HEAD_DIM, HEAD_DIM)] = total[
                    n * BLOCK : (n + 1) * BLOCK
                ]


def attend_back(info, queries, d_out, kv, inverse, qseg, kseg, heads):
    blocks = kseg.shape[0]
    each = heads if blocks <= 8 else 1
    tile = (blocks, each * BLOCK, BLOCK)
    return pl.pallas_call(
        functools.partial(attend_back_kernel, heads, each),
        out_shape=(
            jax.ShapeDtypeStruct(queries.shape, F32),
            jax.ShapeDtypeStruct(kv.shape, F32),
        ),
        in_specs=[pl.BlockSpec(memory_space=pltpu.SMEM)] + [vmem()] * 6,
        out_specs=(vmem(), vmem()),
        scratch_shapes=[pltpu.VMEM(tile, BF16), pltpu.VMEM(tile, F32), pltpu.VMEM(tile, F32)],
        compiler_params=pltpu.CompilerParams(vmem_limit_bytes=(26 if blocks <= 8 else 56) << 20),
        cost_estimate=pl.CostEstimate(
            flops=11 * heads * BLOCK * blocks * BLOCK * HEAD_DIM,
            bytes_accessed=10 << 20,
            transcendentals=2 * heads * BLOCK * blocks * BLOCK,
        ),
        name="attend_back",
    )(info, queries, d_out, kv, inverse, qseg, kseg)


def per_device(
    sizes,
    tokens,
    q_weight,
    key_weight,
    value_weight,
    out_weight,
    gate_weight,
    up_weight,
    down_weight,
    gain_attn_in,
    gain_attn_out,
    gain_mlp_in,
    gain_mlp_out,
    segment_ids,
    block_order,
    cotangent,
):
    tp = sizes["tp"]
    wide = Ring(sizes, ("fsdp", "ctx"))
    near = Ring(sizes, ("ctx",))
    group = 2 * wide.count
    here = lax.axis_index("tp")
    tok = tokens[0]
    count, width = tok.shape
    halves = count // BLOCK
    share = BLOCK // tp
    heads = q_weight.shape[1] // HEAD_DIM
    qcols = q_weight.shape[1]

    split = ("fsdp", "ctx")
    gains_own = jnp.stack([gain_attn_in, gain_attn_out, gain_mlp_in, gain_mlp_out])
    gains_own = jnp.pad(gains_own, ((0, 124), (0, 0))).T
    attn_own = jnp.concatenate(
        [q_weight, key_weight, value_weight, out_weight.T, gains_own], axis=1
    )
    attn_w = lax.all_gather(attn_own, split, axis=0, tiled=True)
    gu_own = jnp.concatenate([gate_weight, after(up_weight, attn_own)], axis=1)
    gu_w = lax.all_gather(after(gu_own, attn_w), split, axis=0, tiled=True)
    down_own = after(down_weight, gu_own).T
    lin_cols = qcols + 2 * HEAD_DIM
    out_cols = lin_cols + out_weight.shape[0]
    qkv_w, out_w = attn_w[:, :lin_cols], attn_w[:, lin_cols:out_cols]
    gains = attn_w[:, out_cols : out_cols + 4].T.astype(F32)
    gain_one, gain_two, gain_three, gain_four = (gains[i] for i in range(4))

    order = block_order[0]
    blocks = order.shape[0]
    stored = jnp.argsort(order).astype(jnp.int32)
    segs = segment_ids[0].reshape(blocks, BLOCK)
    first_block = lax.axis_index("ctx") * halves
    high = lax.dynamic_slice_in_dim(order, first_block, halves)
    qsegs = segs[high]
    low = jnp.sum((segs[None, :, -1] < qsegs[:, :1]).astype(jnp.int32), axis=1)
    bounds = jnp.stack([low, high], axis=1).astype(jnp.int32)
    infos = [jnp.concatenate([bounds[i], stored]) for i in range(halves)]
    info_all = jnp.concatenate([bounds.reshape(-1), stored])
    qseg = qsegs.reshape(count, 1)

    spot = (high[:, None] * BLOCK + jnp.arange(BLOCK, dtype=jnp.int32)[None]).reshape(-1)
    half_dim = HEAD_DIM // 2
    freqs = THETA ** (-jnp.arange(half_dim, dtype=F32) * 2.0 / HEAD_DIM)
    angles = spot.astype(F32)[:, None] * freqs[None, :]
    cosine, sine = jnp.cos(angles), jnp.sin(angles)
    scale = HEAD_DIM**-0.5

    inputs = tok.astype(F32)
    inv_one = inverse_of(inputs)
    normed_attn = (inputs * inv_one * gain_one).astype(BF16)
    lin = dot(normed_attn, qkv_w)
    q_lin = lin[:, :qcols].reshape(count, heads, HEAD_DIM)
    queries = (rotate(q_lin, cosine[:, None], sine[:, None]) * scale).astype(BF16)
    queries = queries.reshape(count, qcols)
    keys = rotate(lin[:, qcols : qcols + HEAD_DIM], cosine, sine).astype(BF16)
    values = lin[:, qcols + HEAD_DIM :].astype(BF16)
    kv_own = jnp.concatenate([keys, values], axis=1)
    kv_move = begun(gather_steps(near, kv_own))
    for _ in range(near.count - 1):
        kv = step(kv_move, queries, qseg, *infos)
    down_move = gather_steps(wide, down_own, attn_w)
    passing = next(down_move)
    down_left = wide.count - 1

    def pass_down(*waits):
        nonlocal passing, down_left
        if down_left:
            passing, down_left = step(down_move, *waits), down_left - 1

    pass_down(kv)

    def rows_of(array, i):
        return lax.slice_in_dim(array, i * BLOCK, (i + 1) * BLOCK)

    def share_of(array, i):
        return lax.dynamic_slice_in_dim(array, i * BLOCK + here * share, share).astype(F32)

    def joined(pieces):
        return jnp.concatenate(pieces, axis=0)

    hops = tp - 1
    both = range(halves)

    def all_steps(parts):
        for _ in range(hops):
            last = [step(part) for part in parts]
        return last

    attended, inverse_sum, sums = [], [], []
    for i in both:
        out, inv = attend(infos[i], rows_of(queries, i), kv, rows_of(qseg, i), segs, heads)
        attended.append(out)
        inverse_sum.append(inv)
        sums.append(tp_scatter(dot_nt(out, out_w).astype(BF16), tp))
        next(sums[i])
    for n in range(hops):
        branch_attn = [step(part) for part in sums]
        if n == 1:
            pass_down(*branch_attn)
    inv_two = [inverse_of(branch) for branch in branch_attn]
    resid = [share_of(tok, i) + branch_attn[i] * inv_two[i] * gain_two for i in both]
    inv_three = [inverse_of(value) for value in resid]
    moves = [tp_gather((resid[i] * inv_three[i] * gain_three).astype(BF16), tp) for i in both]
    for move in moves:
        next(move)
    for n in range(hops - 1):
        sent = [step(move) for move in moves]
    first = step(moves[0])

    gate_lin, up_lin, activ = [None] * halves, [None] * halves, [None] * halves
    gate_lin[0], up_lin[0], activ[0] = gate_up(after(first, sent[-1]), gu_w)
    normed_mlp = [first] + [step(move, activ[0]) for move in moves[1:]]
    while down_left:
        pass_down(activ[0])
    down_w = passing
    sums = [tp_scatter(down(activ[0], down_w), tp)]
    sent = next(sums[0])
    gate_lin[1], up_lin[1], activ[1] = gate_up(after(normed_mlp[1], sent), gu_w)
    sent = step(sums[0], activ[1])
    part = down(after(activ[1], sent), down_w)
    sums.append(tp_scatter(part, tp))
    next(sums[1])
    sent = step(sums[0], part)

    layer_own, grad_four, moves = [], [], []

    def middle(i, branch):
        inv = inverse_of(branch)
        layer_own.append((resid[i] + branch * inv * gain_four).astype(BF16))
        d_branch, d_gain = norm_back(branch, inv, gain_four, share_of(cotangent[0], i))
        grad_four.append(d_gain)
        moves.append(tp_gather(d_branch.astype(BF16), tp))
        return next(moves[i])

    step(sums[1])
    middle(0, step(sums[0]))
    step(sums[1])
    step(moves[0])
    middle(1, step(sums[1]))
    step(moves[0])
    step(moves[1])
    first = step(moves[0])
    sent = step(moves[1])
    d_gate, d_up = [None] * halves, [None] * halves
    d_mlp_low = [first, step(moves[1])]
    grad_down = outer(joined(d_mlp_low), joined(activ), "grad_down")
    d_gate[0], d_up[0] = d_gate_up(after(first, grad_down), down_w, gate_lin[0], up_lin[0])
    part = d_normed_of(after(d_gate[0], grad_down), d_up[0], gu_w)
    sums = [tp_scatter(part, tp)]
    sent = next(sums[0])
    d_gate[1], d_up[1] = d_gate_up(after(d_mlp_low[1], sent), down_w, gate_lin[1], up_lin[1])
    sent = step(sums[0], d_gate[1])
    part = d_normed_of(after(d_gate[1], sent), d_up[1], gu_w)
    sums.append(tp_scatter(part, tp))
    sent = next(sums[1]), step(sums[0], part)
    d_resid, grad_three, grad_two, moves = [], [], [], []

    def middle_back(i, part):
        d_in, d_gain = norm_back(resid[i], inv_three[i], gain_three, part)
        grad_three.append(d_gain)
        d_resid.append(share_of(cotangent[0], i) + d_in)
        d_branch, d_gain = norm_back(branch_attn[i], inv_two[i], gain_two, d_resid[i])
        grad_two.append(d_gain)
        moves.append(tp_gather(d_branch.astype(BF16), tp))
        return next(moves[i])

    normed_all = joined(normed_mlp)
    d_pair = joined(d_gate), joined(d_up)
    grad_gu, mark = outer_pair(after(normed_all, *sent), *d_pair, None, "grad_gate_up")
    sent = middle_back(0, step(sums[0], mark)), step(sums[1], mark)
    grad_gu, mark = outer_pair(after(normed_all, *sent), *d_pair, grad_gu, "grad_gate_up_more")
    sent = step(sums[1], mark), step(moves[0], mark)
    grad_down = lax.psum_scatter(grad_down, split, scatter_dimension=0, tiled=True)
    middle_back(1, step(sums[1]))
    grad_gu = held(grad_gu, grad_down, *sent)
    grad_gu = lax.psum_scatter(grad_gu, split, scatter_dimension=0, tiled=True)
    grad_down = grad_down.astype(F32)
    step(moves[0])
    step(moves[1])
    first = step(moves[0])
    d_attn_low = [first, finish(moves[1], hops - 1)]

    d_attn_all = joined(d_attn_low)
    d_attended = dot(d_attn_all, out_w).astype(BF16)
    d_queries, d_kv = attend_back(
        info_all, queries, d_attended, kv, joined(inverse_sum), qseg, segs, heads
    )
    kv_move = scatter_steps(near, d_kv, BF16)
    d_queries = after(d_queries, next(kv_move))
    d_q_lin = rotate(
        d_queries.reshape(count, heads, HEAD_DIM) * scale, cosine[:, None], -sine[:, None]
    ).astype(BF16)
    d_q_lin = d_q_lin.reshape(count, qcols)
    layer_move = begun(tp_gather(after(jnp.stack(layer_own), d_attn_all), tp))
    passing = step(layer_move, d_kv)
    from_q = dot_nt(after(d_q_lin, passing), qkv_w[:, :qcols])
    passing = step(layer_move, from_q)
    for _ in range(near.count - 1):
        d_kv = step(kv_move, passing)
    d_key_lin = rotate(d_kv[:, :HEAD_DIM], cosine, -sine).astype(BF16)
    d_kv_lin = jnp.concatenate([d_key_lin, d_kv[:, HEAD_DIM:].astype(BF16)], axis=1)
    d_normed_attn = from_q + dot_nt(d_kv_lin, qkv_w[:, qcols:])
    d_normed_low = d_normed_attn.astype(BF16)
    sums = [tp_scatter(rows_of(d_normed_low, i), tp) for i in both]
    sent = [next(part) for part in sums]
    grad_one = jnp.sum(after(d_normed_attn, *sent) * inputs * inv_one, axis=0)
    grad_gains = [grad_one, sum(grad_two), sum(grad_three), sum(grad_four)]
    grad_gains = jnp.stack(grad_gains + [jnp.zeros_like(grad_one)] * 4)
    left, bit = hops, 1
    while bit < tp:
        got = lax.ppermute(grad_gains, "tp", [(i, i ^ bit) for i in range(tp)])
        if left > 1:
            sent, left = [step(part) for part in sums], left - 1
        grad_gains = grad_gains + after(got, *sent)
        bit *= 2
    grad_gains = jnp.pad(grad_gains, ((0, 120), (0, 0))).T
    d_lin = jnp.concatenate([d_q_lin, d_kv_lin], axis=1)
    grad_attn = outer_two(
        normed_attn, d_lin, d_attn_all, joined(attended), grad_gains, "grad_attn"
    )
    grad_attn = held(grad_attn, grad_gu, *sent)
    for _ in range(left):
        sent = [step(part) for part in sums]
    grad_attn = lax.psum_scatter(grad_attn, split, scatter_dimension=0, tiled=True)
    grad_gu = grad_gu.astype(F32)
    moves = []
    for i in both:
        own = share_of(tok, i)
        d_in, unused = norm_back(own, inverse_of(own), gain_one, sent[i])
        moves.append(begun(tp_gather((d_resid[i] + d_in).astype(BF16), tp, F32)))
    for n in range(hops):
        grad_tokens = [step(move) for move in moves]
        if n == hops - 2:
            layer_out = step(layer_move, *grad_tokens)
    grad_gains = grad_attn[:, out_cols : out_cols + 4].T.astype(F32)
    grad_out = grad_attn[:, lin_cols:out_cols].astype(F32)
    grad_qkv = grad_attn[:, :lin_cols]

    return (
        layer_out.reshape(1, count, width),
        joined(grad_tokens)[None],
        grad_qkv[:, :qcols].astype(F32),
        grad_qkv[:, qcols : qcols + HEAD_DIM].astype(F32),
        grad_qkv[:, qcols + HEAD_DIM :].astype(F32),
        grad_out.T,
        grad_gu[:, : gate_weight.shape[1]],
        grad_gu[:, gate_weight.shape[1] :],
        grad_down.T,
        grad_gains[0],
        grad_gains[1],
        grad_gains[2],
        grad_gains[3],
    )


def solution(mesh):
    sizes = dict(mesh.shape)
    split = ("fsdp", "ctx")
    rows, cols = P(split, "tp"), P("tp", split)
    acts, ids = P("fsdp", "ctx", None), P("fsdp", None)
    return jax.shard_map(
        functools.partial(per_device, sizes),
        mesh=mesh,
        in_specs=(acts, rows, rows, rows, cols, rows, rows, cols)
        + (P(split),) * 4
        + (ids, ids, acts),
        out_specs=(acts, acts, rows, rows, rows, cols, rows, rows, cols) + (P(split),) * 4,
        check_vma=False,
    )
```
